32 devices in a mesh: ep: 8 (over z, x), tp: 4 (over y, core).
Axes of the slice: x: 2, y: 2, z: 4, core: 2. Of those that a mesh axis runs over, the one named last changes fastest.
Arguments:
- resid: bfloat16 [2048, 1536], P('ep'), may hold values from -6 to 6
- context: bfloat16 [2048, 1536], P('ep', 'tp'), may hold values from -6 to 6
- w_out: bfloat16 [1536, 1536], P('tp'), may hold values from -0.15625 to 0.15625
- pre_gain: bfloat16 [1536], replicated, may hold values from 0.5 to 1.5
- final_gain: bfloat16 [1536], replicated, may hold values from 0.5 to 1.5
- w_router: bfloat16 [1536, 40], replicated, may hold values from -0.03491211 to 0.03491211
- expert_ids: int32 [2048, 8], P('ep'), may hold values from 0 to 39, all different within a row; in each aligned block of 256 rows (0 to 255, 256 to 511, ...) at most 80 rows name the same one
- slot_expert: int32 [40], replicated, may hold values from 0 to 39, as said below
- copy_pick: int32 [8, 40], P('ep'), may hold values from 0 to 7
- w_gate: bfloat16 [40, 1536, 512], P('ep', None, 'tp'), may hold values from -0.15625 to 0.15625
- w_up: bfloat16 [40, 1536, 512], P('ep', None, 'tp'), may hold values from -0.15625 to 0.15625
- w_down: bfloat16 [40, 512, 1536], P('ep', 'tp'), may hold values from -0.25 to 0.25
Outputs:
- layer_out: bfloat16 [2048, 1536], P('ep')
The draws below stay inside these ranges and needn't reach their ends.
Inputs may be any that keep to these rules, and one draw needn't show every extreme that they name: `expert_ids`: each row names 8 different experts; among the rows of one index of ep no expert is named by more than 80 rows, a bound that some block reaches of them. `slot_expert`: every expert is held by at least one slot.
All inputs are finite; a program needn't handle non-finite values.
Results may differ from the reference program's by a relative error of at most 0.012.
Values may be sent and summed in bfloat16 or wider, within the bound.
No kernel may reach another device: no remote copies, remote signals or barrier semaphores. Data moves between devices by JAX's collectives and lax.ppermute only.
A program may use at most 128 MiB of HBM per device.

```python
import math
import jax
import jax.numpy as jnp
import numpy as np
from jax import lax

D = 1536
FF = 512
EXPERTS = 40
TOP = 8
ROWS_DEV = 256
CAP = 80
SLOTS = 40
ROWS = 2048
N_EP = 8
N_TP = 4


def draw_slot_expert(key, part):
    order = jax.random.permutation(key, SLOTS)
    return (order % EXPERTS).astype(jnp.int32)


def touch_ends(drawn, key, smallest, high):
    shape = drawn.shape
    index_at = [jax.random.randint(jax.random.fold_in(key, axis), (), 0, shape[axis]) for axis in range(len(shape))]
    drawn = drawn.at[tuple(index_at)].set(smallest)
    longest = shape.index(max(shape))
    index_at[longest] = (index_at[longest] + 1) % shape[longest]
    return drawn.at[tuple(index_at)].set(high)


def block_scale(key, shape, shards, smallest, high):
    def one(dim, parts):
        draws = jax.random.uniform(jax.random.fold_in(jax.random.fold_in(key, 6), dim), (parts,), jnp.float32, smallest / len(shards), high / len(shards))
        return jnp.repeat(jnp.exp(draws), shape[dim] // parts).reshape((-1,) + (1,) * (len(shape) - dim - 1))

    factor_of = one(*shards[0])
    for cut in shards[1:]:
        factor_of = factor_of * one(*cut)
    return factor_of


def deal_out(key, own, number, rows, count, top, most, slope):
    ranking = jax.random.permutation(key, count)
    heavy_load, common = load_shares(count, rows * top, most, slope, True), load_shares(count, rows * top, most, slope, False)
    places = jnp.arange(count)

    def named(lengths, offset_by):
        used = int((lengths > 0).sum())
        fixed = max(1, used // 4)
        shifted = fixed + (places - fixed + offset_by * (used - fixed)) % max(1, count - fixed)
        return jnp.zeros((count,), jnp.int32).at[ranking[jnp.where(places < fixed, places, shifted)]].set(jnp.asarray(lengths, jnp.int32))

    lengths = jnp.where(number % 4 == 0, named(heavy_load, number // 4), named(common, number - number // 4 - 1))
    mixed = jax.random.permutation(jax.random.fold_in(own, 3), count)
    donor, sink = mixed[0:count // 2 * 2:2], mixed[1:count // 2 * 2:2]
    margin = jnp.minimum(lengths[donor] - 1, most - lengths[sink]) // 2
    margin = jnp.where((donor == ranking[0]) | (sink == ranking[0]) | (lengths[sink] == 0), 0, jnp.maximum(margin, 0))
    shifted = jax.random.randint(jax.random.fold_in(own, 4), (count // 2,), 0, 1 << 20) % (margin + 1)
    lengths = lengths.at[donor].add(-shifted).at[sink].add(shifted)
    members = jnp.searchsorted(jnp.cumsum(lengths), jnp.arange(rows * top), side="right").astype(jnp.int32)
    listing = members.reshape(top, rows).T
    listing = listing[jax.random.permutation(jax.random.fold_in(own, 1), rows)]
    offset_by = jax.random.randint(jax.random.fold_in(own, 2), (rows, 1), 0, top)
    return jnp.take_along_axis(listing, (jnp.arange(top)[None, :] + offset_by) % top, axis=1)


def load_shares(number_of, total, most, skew, full):
    loads = [(1 << 20) // math.isqrt(grade ** skew) + 1 for grade in range(1, number_of + 1)]
    largest = most if full else min(most, max(-(-total // number_of), total * loads[0] // sum(loads)))
    least = 1 if total - largest >= number_of - 1 else 0
    counts, surplus = [largest] + [least] * (number_of - 1), total - largest - least * (number_of - 1)
    while surplus > 0:
        free = [i for i in range(1, number_of) if counts[i] < largest] or [i for i in range(1, number_of) if counts[i] < most]
        mass, budget = sum([loads[i] for i in free]), surplus
        for i in free:
            more = min(most - counts[i], max(1, budget * loads[i] // mass), surplus)
            counts[i] = counts[i] + more
            surplus = surplus - more
    return np.array(counts)


def bell_draw(rng, extent, width, most, shards=(), kind=jnp.bfloat16):
    factor_of = block_scale(rng, extent, shards, -0.22, 0.18) if shards else 1.0
    drawn = jax.random.normal(rng, extent, jnp.float32) * width * factor_of
    return jnp.minimum(jnp.maximum(drawn, -most), most).astype(kind)


def setup_inputs(seed: int = 0) -> dict:
    seeds = jax.random.split(jax.random.key(seed), 13)
    resid = bell_draw(seeds[0], (ROWS, D), 1.0, 6.0, ((0, 8),))
    context = bell_draw(seeds[1], (ROWS, D), 1.0, 6.0, ((0, 8), (1, 4)))
    w_out = bell_draw(seeds[2], (D, D), D ** -0.5, 0.15625, ((0, 4),))
    pre_gain = jnp.clip(1.0 + 0.1 * jax.random.normal(seeds[3], (D,), jnp.float32), 0.5, 1.5).astype(jnp.bfloat16)
    final_gain = jnp.clip(1.0 + 0.1 * jax.random.normal(seeds[4], (D,), jnp.float32), 0.5, 1.5).astype(jnp.bfloat16)
    w_router = jnp.clip(jax.random.uniform(seeds[5], (D, EXPERTS), jnp.float32, -0.03491211, 0.03491211), -0.03491211, 0.03491211).astype(jnp.bfloat16)
    expert_ids_keys = jax.random.split(jax.random.fold_in(seeds[6], 1), ROWS // ROWS_DEV)
    expert_ids_turns = jax.random.permutation(jax.random.fold_in(seeds[6], 3), ROWS // ROWS_DEV)
    expert_ids = jax.vmap(lambda own, number: deal_out(jax.random.fold_in(seeds[6], 2), own, number, ROWS_DEV, EXPERTS, TOP, CAP, 1))(expert_ids_keys, expert_ids_turns).reshape((ROWS, TOP))
    slot_expert = draw_slot_expert(jax.random.fold_in(seeds[12], 71), 0)
    copy_pick = touch_ends(jax.random.randint(seeds[8], (N_EP, EXPERTS), 0, 8), jax.random.fold_in(seeds[8], 1), 0, 7).astype(jnp.int32)
    w_gate = bell_draw(seeds[9], (SLOTS, D, FF), D ** -0.5, 0.15625, ((0, 8), (2, 4)))
    w_up = bell_draw(seeds[10], (SLOTS, D, FF), D ** -0.5, 0.15625, ((0, 8), (2, 4)))
    w_down = bell_draw(seeds[11], (SLOTS, FF, D), FF ** -0.5, 0.25, ((0, 8), (1, 4)))
    return dict(resid=resid, context=context, w_out=w_out, pre_gain=pre_gain, final_gain=final_gain, w_router=w_router, expert_ids=expert_ids, slot_expert=slot_expert, copy_pick=copy_pick, w_gate=w_gate, w_up=w_up, w_down=w_down)


EPSILON = 1e-06

def rms_scaled(values, gain):
    mean_square = lax.optimization_barrier(jnp.mean(values * values, axis=-1, keepdims=True))
    return values * lax.rsqrt(mean_square + EPSILON) * gain.astype(jnp.float32)

def slot_of_pick(slot_expert, copy_pick, experts):
    count = slot_expert.shape[0]
    order = jnp.arange(count, dtype=jnp.int32)
    same = slot_expert[:, None] == slot_expert[None, :]
    before = order[None, :] < order[:, None]
    rank = lax.optimization_barrier(jnp.sum((same & before).astype(jnp.int32), axis=1))
    holds = slot_expert[None, :] == jnp.arange(experts, dtype=jnp.int32)[:, None]
    copies = lax.optimization_barrier(jnp.sum(holds.astype(jnp.int32), axis=1))
    wanted = copy_pick % copies[None, :]
    match = holds[None, :, :] & (rank[None, None, :] == wanted[:, :, None])
    return lax.optimization_barrier(jnp.sum(match.astype(jnp.int32) * order[None, None, :], axis=2))

def reference(resid, context, w_out, pre_gain, final_gain, w_router, expert_ids, slot_expert, copy_pick, w_gate, w_up, w_down):
    total_rows = resid.shape[0]
    attention = jnp.dot(context, w_out, preferred_element_type=jnp.float32)
    middle = resid.astype(jnp.float32) + attention
    normed = rms_scaled(middle, pre_gain).astype(jnp.bfloat16)
    logits = jnp.dot(normed, w_router, preferred_element_type=jnp.float32)
    chosen = jnp.take_along_axis(logits, expert_ids, axis=1)
    raised = jnp.exp(chosen)
    weights = (raised / lax.optimization_barrier(jnp.sum(raised, axis=1, keepdims=True))).astype(jnp.bfloat16)
    table = slot_of_pick(slot_expert, copy_pick, EXPERTS)
    owner = (jnp.arange(total_rows, dtype=jnp.int32) // ROWS_DEV).astype(jnp.int32)
    slot = table[owner[:, None], expert_ids].reshape(-1)
    flat_row = (jnp.arange(total_rows * TOP, dtype=jnp.int32) // TOP).astype(jnp.int32)
    flat_weight = weights.reshape(-1).astype(jnp.float32)
    quarter = FF // N_TP
    capacity = N_EP * CAP

    def per_slot(mixture, number):
        hits = slot == number
        filled = jnp.sum(hits.astype(jnp.int32))
        picked = jnp.nonzero(hits, size=capacity, fill_value=0)[0].astype(jnp.int32)
        valid = jnp.arange(capacity, dtype=jnp.int32) < filled
        rows_in = normed[flat_row[picked]]
        gate = jnp.dot(rows_in, w_gate[number], preferred_element_type=jnp.float32)
        upper = jnp.dot(rows_in, w_up[number], preferred_element_type=jnp.float32)
        hidden = (jax.nn.silu(gate) * upper).astype(jnp.bfloat16)
        down = w_down[number]
        summed = jnp.zeros((capacity, D), jnp.float32)
        for lane in range(N_TP):
            piece = jnp.dot(hidden[:, lane * quarter:(lane + 1) * quarter], down[lane * quarter:(lane + 1) * quarter], preferred_element_type=jnp.float32)
            summed = summed + lax.optimization_barrier(piece.astype(jnp.bfloat16)).astype(jnp.float32)
        scale = jnp.where(valid, flat_weight[picked], jnp.float32(0.0))
        mixture = mixture.at[flat_row[picked]].add(summed * scale[:, None])
        return (mixture, None)
    mixture, _ = lax.scan(per_slot, jnp.zeros((total_rows, D), jnp.float32), jnp.arange(SLOTS, dtype=jnp.int32))
    return rms_scaled(middle + mixture, final_gain).astype(jnp.bfloat16)
```

```python
import functools

import jax
import jax.numpy as jnp
from jax import lax
from jax.experimental import pallas as pl
from jax.experimental.pallas import tpu as pltpu
from jax.sharding import PartitionSpec as P

EPSILON = 1e-06
CHUNKS = 2
LANES = 128
ROW_BLOCK = 512


def slot_of_pick(slot_expert, copy_pick, experts):
    count = slot_expert.shape[0]
    order = jnp.arange(count, dtype=jnp.int32)
    same = slot_expert[:, None] == slot_expert[None, :]
    before = order[None, :] < order[:, None]
    rank = jnp.sum((same & before).astype(jnp.int32), axis=1)
    holds = slot_expert[None, :] == jnp.arange(experts, dtype=jnp.int32)[:, None]
    copies = jnp.sum(holds.astype(jnp.int32), axis=1)
    wanted = copy_pick % copies[None, :]
    match = holds[None, :, :] & (rank[None, None, :] == wanted[:, :, None])
    return jnp.sum(match.astype(jnp.int32) * order[None, None, :], axis=2)


def rms_scaled(values, gain):
    mean_square = jnp.mean(values * values, axis=-1, keepdims=True)
    return values * lax.rsqrt(mean_square + EPSILON) * gain.astype(jnp.float32)


def turn(value, step):
    count = lax.axis_size("ep")
    return lax.ppermute(value, "ep", [(i, (i + 2 * step) % count) for i in range(count)])


def flip_inner(value):
    return lax.ppermute(value, "ep", [(i, i ^ 1) for i in range(lax.axis_size("ep"))])


def flip_upper(value):
    return lax.ppermute(value, "tp", [(i, i ^ 2) for i in range(lax.axis_size("tp"))])


def flip_lower(value):
    return lax.ppermute(value, "tp", [(i, i ^ 1) for i in range(lax.axis_size("tp"))])


VMEM = pl.BlockSpec(memory_space=pltpu.VMEM)
SMEM = pl.BlockSpec(memory_space=pltpu.SMEM)


def attend_kernel(place_ref, context_ref, w_ref, send_ref, keep_ref):
    place = place_ref[0]
    quarter = send_ref.shape[1]
    rows = []
    for lower in (1, 0):
        for upper in (0, 1):
            start = pl.multiple_of((place ^ (upper * 2 + lower)) * quarter, quarter)
            rows.append(context_ref[pl.ds(start, quarter), :])
    rows = jnp.concatenate(rows, axis=0)
    width = w_ref.shape[1]
    tile = 512 if width % 512 == 0 else width
    for left in range(0, width, tile):
        out = jnp.dot(rows, w_ref[:, left : left + tile], preferred_element_type=jnp.float32)
        for upper in (0, 1):
            send_ref[upper, :, left : left + tile] = out[
                upper * quarter : (upper + 1) * quarter
            ].astype(jnp.bfloat16)
            keep_ref[upper, :, left : left + tile] = out[
                (upper + 2) * quarter : (upper + 3) * quarter
            ]


def attend(place, context, w_out):
    rows, _ = context.shape
    width = w_out.shape[1]
    quarter = rows // 4
    return pl.pallas_call(
        attend_kernel,
        out_shape=(
            jax.ShapeDtypeStruct((2, quarter, width), jnp.bfloat16),
            jax.ShapeDtypeStruct((2, quarter, width), jnp.float32),
        ),
        in_specs=[SMEM, VMEM, VMEM],
        out_specs=(VMEM, VMEM),
        name="attend",
    )(place, context, w_out)


def norm_kernel(place_ref, keep_ref, lower_ref, upper_ref, resid_ref, gain_ref, middle_ref, normed_ref):
    attention = (
        keep_ref[0] + lower_ref[0].astype(jnp.float32) + upper_ref[...].astype(jnp.float32)
    )
    middle = resid_ref[...].astype(jnp.float32) + attention
    middle_ref[...] = middle
    normed_ref[...] = rms_scaled(middle, gain_ref[...]).astype(jnp.bfloat16)


def norm_rows(place, keep, from_lower, from_upper, resid, gain, number):
    rows, width = from_upper.shape
    chunks = keep.shape[1] // rows
    return pl.pallas_call(
        norm_kernel,
        out_shape=(
            jax.ShapeDtypeStruct((rows, width), jnp.float32),
            jax.ShapeDtypeStruct((rows, width), jnp.bfloat16),
        ),
        grid_spec=pltpu.PrefetchScalarGridSpec(
            num_scalar_prefetch=1,
            grid=(1,),
            in_specs=[
                pl.BlockSpec((1, rows, width), lambda i, p: (0, number, 0)),
                pl.BlockSpec((1, rows, width), lambda i, p: (0, number, 0)),
                pl.BlockSpec((rows, width), lambda i, p: (0, 0)),
                pl.BlockSpec((rows, width), lambda i, p: (p[0] * chunks + number, 0)),
                pl.BlockSpec((1, width), lambda i, p: (0, 0)),
            ],
            out_specs=[
                pl.BlockSpec((rows, width), lambda i, p: (0, 0)),
                pl.BlockSpec((rows, width), lambda i, p: (0, 0)),
            ],
        ),
        name="norm_rows",
    )(place, keep, from_lower, from_upper, resid, gain)


def expert_kernel(*refs):
    pieces = refs[:4]
    ids_ref, router_ref, gate_ref, up_ref, down_ref, out_ref, rows_ref, hidden_ref = refs[4:]
    held, _, units = gate_ref.shape
    start = 0
    for piece in pieces:
        rows_ref[start : start + piece.shape[0]] = piece[...]
        start += piece.shape[0]
    block = min(ROW_BLOCK, start)

    def one_block(number):
        at = pl.ds(pl.multiple_of(number * block, block), block)
        rows = rows_ref[at, :]
        logits = jnp.dot(rows, router_ref[...], preferred_element_type=jnp.float32)
        lane = lax.broadcasted_iota(jnp.int32, (1, LANES), 1)
        ids = ids_ref[at, :]
        hit = ids[:, 0:1] == lane
        for choice in range(1, ids.shape[1]):
            hit = hit | (ids[:, choice : choice + 1] == lane)
        raised = jnp.where(hit, jnp.exp(logits), 0.0)
        weights = raised / jnp.sum(raised, axis=1, keepdims=True)
        weights = weights.astype(jnp.bfloat16).astype(jnp.float32)
        for slot in range(held):
            both = jnp.concatenate([gate_ref[slot], up_ref[slot]], axis=1)
            out = jnp.dot(rows, both, preferred_element_type=jnp.float32)
            gate, upper = out[:, :units], out[:, units:]
            hidden = jax.nn.silu(gate) * upper * weights[:, slot : slot + 1]
            hidden_ref[:, slot * units : (slot + 1) * units] = hidden.astype(jnp.bfloat16)
        width = out_ref.shape[1]
        tile = 512 if width % 512 == 0 else width
        for left in range(0, width, tile):
            out_ref[at, left : left + tile] = jnp.dot(
                hidden_ref[...],
                down_ref[:, left : left + tile],
                preferred_element_type=jnp.float32,
            ).astype(jnp.bfloat16)

    if start == block:
        one_block(0)
    else:
        pl.loop(0, start // block)(one_block)


def expert_rows(pieces, ids, router, w_gate, w_up, w_down):
    held, width, units = w_gate.shape
    rows = sum(p.shape[0] for p in pieces)
    block = min(ROW_BLOCK, rows)
    return pl.pallas_call(
        expert_kernel,
        out_shape=jax.ShapeDtypeStruct((rows, width), jnp.bfloat16),
        in_specs=[VMEM] * (len(pieces) + 5),
        out_specs=VMEM,
        scratch_shapes=[
            pltpu.VMEM((rows, width), jnp.bfloat16),
            pltpu.VMEM((block, held * units), jnp.bfloat16),
        ],
        compiler_params=pltpu.CompilerParams(vmem_limit_bytes=32 << 20),
        cost_estimate=pl.CostEstimate(
            flops=2 * rows * width * (3 * held * units + LANES),
            bytes_accessed=4 * rows * width + 6 * held * width * units,
            transcendentals=rows * (held * units + LANES),
        ),
        name="expert_rows",
    )(*pieces, ids, router, w_gate, w_up, w_down)


def gather_pieces(rows):
    outer = lax.axis_size("ep") // 2
    half = rows.shape[0] // 2
    ring = [rows] + [turn(rows, step) for step in range(1, outer)]
    first = jnp.concatenate([r[:half] for r in ring], axis=0)
    second = jnp.concatenate([r[half:] for r in ring], axis=0)
    first = jnp.concatenate([first, flip_inner(first)], axis=0)
    second = jnp.concatenate([second, flip_upper(second)], axis=0)
    return [first, flip_upper(first), second, flip_inner(second)]


def wide(value):
    return value.astype(jnp.float32)


def short(value):
    return value.astype(jnp.bfloat16)


def sum_back(own, from_lower):
    outer = lax.axis_size("ep") // 2
    rows = own.shape[0]
    part, quarter, eighth = rows // 2, rows // 4, rows // 8
    half = eighth // outer

    def cut(value, start, size):
        return wide(lax.slice_in_dim(value, start, start + size, axis=0))

    def two(start, size):
        return cut(own, start, size) + cut(from_lower, start, size)

    got_first = flip_upper(short(two(quarter, quarter)))
    got_second = flip_inner(short(two(part + quarter, quarter)))
    next_first = flip_inner(short(two(eighth, eighth) + cut(got_first, eighth, eighth)))
    next_second = flip_upper(short(two(part + eighth, eighth) + cut(got_second, eighth, eighth)))

    def block(number):
        at = number * half
        return jnp.concatenate(
            [
                two(at, half) + cut(got_first, at, half) + cut(next_first, at, half),
                two(part + at, half) + cut(got_second, at, half) + cut(next_second, at, half),
            ],
            axis=0,
        )

    total = block(0)
    for step in range(1, outer):
        total = total + wide(turn(short(block(step)), -step))
    return total


def gather_ids(ids):
    outer = lax.axis_size("ep") // 2
    quarter, choose = ids.shape
    half = quarter // (CHUNKS * 2)
    ring = jnp.stack([ids] + [turn(ids, step) for step in range(1, outer)])
    ring = jnp.stack([ring, flip_inner(ring)])
    ring = jnp.stack([ring, flip_upper(ring)])
    ring = jnp.stack([ring, flip_lower(ring)])
    ring = ring.reshape(2, 2, 2, outer, CHUNKS, 2, half, choose)
    first = jnp.transpose(ring[:, :, :, :, :, 0], (4, 0, 1, 2, 3, 5, 6))
    second = jnp.transpose(ring[:, :, :, :, :, 1], (4, 0, 2, 1, 3, 5, 6))
    both = jnp.stack([first, second], axis=2)
    return both.reshape(CHUNKS, 2, -1, choose)


def local(
    resid,
    context,
    w_out,
    pre_gain,
    final_gain,
    w_router,
    expert_ids,
    slot_expert,
    copy_pick,
    w_gate,
    w_up,
    w_down,
):
    held, width, units = w_gate.shape
    row_count = resid.shape[0]
    choose = expert_ids.shape[1]
    experts = w_router.shape[1]
    slots = slot_expert.shape[0]
    quarter = row_count // 4
    rows = quarter // CHUNKS
    me = lax.axis_index("ep")
    place = lax.axis_index("tp").astype(jnp.int32).reshape(1)

    send, keep = attend(place, context, w_out)

    table = slot_of_pick(slot_expert, copy_pick, experts)[0]
    my_ids = lax.dynamic_slice_in_dim(expert_ids, place[0] * quarter, quarter, axis=0)
    onehot = my_ids[:, :, None] == jnp.arange(experts, dtype=jnp.int32)[None, None, :]
    slot = jnp.sum(jnp.where(onehot, table[None, None, :], 0), axis=2)
    slot = (gather_ids(slot) - me * held) % slots
    rolled = jnp.roll(slot_expert, -me * held)
    column = jnp.arange(experts, dtype=jnp.int32)[:, None] == rolled[None, :]
    router = jnp.dot(w_router, column.astype(jnp.bfloat16), preferred_element_type=jnp.float32)
    router = jnp.pad(router.astype(jnp.bfloat16), ((0, 0), (0, LANES - slots)))
    down = w_down.reshape(held * units, width)

    got = flip_lower(send)
    middles, normeds = [], []
    for number in range(CHUNKS):
        at = slice(number * rows, (number + 1) * rows)
        upper = flip_upper(short(keep[1, at] + wide(got[1, at])))
        middle, normed = norm_rows(place, keep, got, upper, resid, pre_gain.reshape(1, -1), number)
        middles.append(middle)
        normeds.append(normed)

    results = []
    for number in range(CHUNKS):
        pieces = gather_pieces(normeds[number])
        other = [flip_lower(p) for p in pieces]
        own = expert_rows(pieces, slot[number, 0], router, w_gate, w_up, down)
        away = expert_rows(other, slot[number, 1], router, w_gate, w_up, down)
        total = sum_back(own, flip_lower(away))
        results.append(rms_scaled(middles[number] + total, final_gain).astype(jnp.bfloat16))
    result = jnp.concatenate(results, axis=0)
    return lax.all_gather(result, "tp", tiled=True)


def solution(mesh):
    return jax.shard_map(
        local,
        mesh=mesh,
        in_specs=(
            P("ep", None),
            P("ep", "tp"),
            P("tp", None),
            P(),
            P(),
            P(),
            P("ep", None),
            P(),
            P("ep", None),
            P("ep", None, "tp"),
            P("ep", None, "tp"),
            P("ep", "tp", None),
        ),
        out_specs=P("ep", None),
        check_vma=False,
    )
```

```python
import functools

import jax
import jax.numpy as jnp
from jax import lax
from jax.experimental import pallas as pl
from jax.experimental.pallas import tpu as pltpu
from jax.sharding import PartitionSpec as P

EPSILON = 1e-06
CHUNKS = 2
LANES = 128
ROW_BLOCK = 512


def slot_of_pick(slot_expert, copy_pick, experts):
    count = slot_expert.shape[0]
    order = jnp.arange(count, dtype=jnp.int32)
    same = slot_expert[:, None] == slot_expert[None, :]
    before = order[None, :] < order[:, None]
    rank = jnp.sum((same & before).astype(jnp.int32), axis=1)
    holds = slot_expert[None, :] == jnp.arange(experts, dtype=jnp.int32)[:, None]
    copies = jnp.sum(holds.astype(jnp.int32), axis=1)
    wanted = copy_pick % copies[None, :]
    match = holds[None, :, :] & (rank[None, None, :] == wanted[:, :, None])
    return jnp.sum(match.astype(jnp.int32) * order[None, None, :], axis=2)


def rms_scaled(values, gain):
    mean_square = jnp.mean(values * values, axis=-1, keepdims=True)
    return values * lax.rsqrt(mean_square + EPSILON) * gain.astype(jnp.float32)


def turn(value, step):
    count = lax.axis_size("ep")
    return lax.ppermute(value, "ep", [(i, (i + 2 * step) % count) for i in range(count)])


def flip_inner(value):
    return lax.ppermute(value, "ep", [(i, i ^ 1) for i in range(lax.axis_size("ep"))])


def flip_upper(value):
    return lax.ppermute(value, "tp", [(i, i ^ 2) for i in range(lax.axis_size("tp"))])


def flip_lower(value):
    return lax.ppermute(value, "tp", [(i, i ^ 1) for i in range(lax.axis_size("tp"))])


VMEM = pl.BlockSpec(memory_space=pltpu.VMEM)
SMEM = pl.BlockSpec(memory_space=pltpu.SMEM)
ANY = pl.BlockSpec(memory_space=pl.ANY)


def attend_kernel(place_ref, context_ref, w_ref, send_ref, keep_ref):
    place = place_ref[0]
    quarter = send_ref.shape[1]
    rows = []
    for lower in (1, 0):
        for upper in (0, 1):
            start = pl.multiple_of((place ^ (upper * 2 + lower)) * quarter, quarter)
            rows.append(context_ref[pl.ds(start, quarter), :])
    rows = jnp.concatenate(rows, axis=0)
    width = w_ref.shape[1]
    tile = 512 if width % 512 == 0 else width
    for left in range(0, width, tile):
        out = jnp.dot(rows, w_ref[:, left : left + tile], preferred_element_type=jnp.float32)
        for upper in (0, 1):
            send_ref[upper, :, left : left + tile] = out[
                upper * quarter : (upper + 1) * quarter
            ].astype(jnp.bfloat16)
            keep_ref[upper, :, left : left + tile] = out[
                (upper + 2) * quarter : (upper + 3) * quarter
            ]


def attend(place, context, w_out):
    rows, _ = context.shape
    width = w_out.shape[1]
    quarter = rows // 4
    return pl.pallas_call(
        attend_kernel,
        out_shape=(
            jax.ShapeDtypeStruct((2, quarter, width), jnp.bfloat16),
            jax.ShapeDtypeStruct((2, quarter, width), jnp.float32),
        ),
        in_specs=[SMEM, VMEM, VMEM],
        out_specs=(VMEM, VMEM),
        compiler_params=pltpu.CompilerParams(vmem_limit_bytes=16 << 20),
        name="attend",
    )(place, context, w_out)


def norm_kernel(
    place_ref,
    keep_ref,
    lower_ref,
    upper_ref,
    resid_ref,
    gain_ref,
    ids_ref,
    router_ref,
    slot_hot_ref,
    middle_ref,
    row_ref,
):
    attention = (
        keep_ref[0] + lower_ref[0].astype(jnp.float32) + upper_ref[...].astype(jnp.float32)
    )
    middle = resid_ref[...].astype(jnp.float32) + attention
    middle_ref[...] = middle
    width = middle.shape[1]
    normed = rms_scaled(middle, gain_ref[...]).astype(jnp.bfloat16)
    row_ref[:, :width] = normed
    logits = jnp.dot(normed, router_ref[...], preferred_element_type=jnp.float32)
    expert = lax.broadcasted_iota(jnp.int32, logits.shape, 1)
    ids = ids_ref[...]
    hit = ids[:, 0:1] == expert
    for choice in range(1, ids.shape[1]):
        hit = hit | (ids[:, choice : choice + 1] == expert)
    raised = jnp.where(hit, jnp.exp(logits), 0.0)
    weights = (raised / jnp.sum(raised, axis=1, keepdims=True)).astype(jnp.bfloat16)
    row_ref[:, width:] = jnp.dot(
        weights, slot_hot_ref[...], preferred_element_type=jnp.float32
    ).astype(jnp.bfloat16)


def norm_rows(place, keep, from_lower, from_upper, resid, gain, ids, router, slot_hot, number):
    rows, width = from_upper.shape
    chunks = keep.shape[1] // rows
    extra = slot_hot.shape[1]

    def whole(array):
        return pl.BlockSpec(array.shape, lambda i, p: (0, 0))

    def mine(array):
        return pl.BlockSpec((rows, array.shape[1]), lambda i, p: (p[0] * chunks + number, 0))

    return pl.pallas_call(
        norm_kernel,
        out_shape=(
            jax.ShapeDtypeStruct((rows, width), jnp.float32),
            jax.ShapeDtypeStruct((rows, width + extra), jnp.bfloat16),
        ),
        grid_spec=pltpu.PrefetchScalarGridSpec(
            num_scalar_prefetch=1,
            grid=(1,),
            in_specs=[
                pl.BlockSpec((1, rows, width), lambda i, p: (0, number, 0)),
                pl.BlockSpec((1, rows, width), lambda i, p: (0, number, 0)),
                whole(from_upper),
                mine(resid),
                whole(gain),
                mine(ids),
                whole(router),
                whole(slot_hot),
            ],
            out_specs=[
                pl.BlockSpec((rows, width), lambda i, p: (0, 0)),
                pl.BlockSpec((rows, width + extra), lambda i, p: (0, 0)),
            ],
        ),
        compiler_params=pltpu.CompilerParams(vmem_limit_bytes=16 << 20),
        name="norm_rows",
    )(place, keep, from_lower, from_upper, resid, gain, ids, router, slot_hot)


def load_kernel(gate_hbm, up_hbm, down_hbm, both_ref, down_ref, sems):
    units = gate_hbm.shape[2]
    copies = [
        pltpu.make_async_copy(gate_hbm, both_ref.at[:, :, pl.ds(0, units)], sems.at[0]),
        pltpu.make_async_copy(up_hbm, both_ref.at[:, :, pl.ds(units, units)], sems.at[1]),
        pltpu.make_async_copy(down_hbm, down_ref, sems.at[2]),
    ]
    for copy in copies:
        copy.start()
    for copy in copies:
        copy.wait()


def load_weights(w_gate, w_up, w_down):
    held, width, units = w_gate.shape
    return pl.pallas_call(
        load_kernel,
        out_shape=(
            pltpu.VMEM((held, width, 2 * units), jnp.bfloat16),
            pltpu.VMEM((held * units, width), jnp.bfloat16),
        ),
        in_specs=[ANY] * 3,
        out_specs=(VMEM, VMEM),
        scratch_shapes=[pltpu.SemaphoreType.DMA((3,))],
        compiler_params=pltpu.CompilerParams(vmem_limit_bytes=2 << 20),
        name="load_weights",
    )(w_gate, w_up, w_down)


def expert_kernel(
    first_ref,
    near_ref,
    far_ref,
    other_near_ref,
    other_far_ref,
    both_ref,
    down_ref,
    near_out,
    far_out,
    other_near_out,
    other_far_out,
    rows_ref,
    hidden_ref,
):
    held, width, units = both_ref.shape
    units = units // 2
    start = 0
    for piece in (near_ref, far_ref, other_near_ref, other_far_ref):
        rows_ref[start : start + piece.shape[0]] = piece[...]
        start += piece.shape[0]
    block = min(ROW_BLOCK, start)
    extra = rows_ref.shape[1] - width
    mine = lax.broadcasted_iota(jnp.int32, (extra, LANES), 1) + first_ref[0]
    mine = (lax.broadcasted_iota(jnp.int32, (extra, LANES), 0) == mine).astype(jnp.bfloat16)
    tile = 512 if width % 512 == 0 else width

    def one_block(at):
        weights = jnp.dot(rows_ref[at, width:], mine, preferred_element_type=jnp.float32)
        for slot in range(held):
            out = jnp.dot(rows_ref[at, :width], both_ref[slot], preferred_element_type=jnp.float32)
            gate, upper = out[:, :units], out[:, units:]
            hidden = jax.nn.silu(gate) * upper * weights[:, slot : slot + 1]
            hidden_ref[:, slot * units : (slot + 1) * units] = hidden.astype(jnp.bfloat16)
        for left in range(0, width, tile):
            out = jnp.dot(
                hidden_ref[...],
                down_ref[:, left : left + tile],
                preferred_element_type=jnp.float32,
            ).astype(jnp.bfloat16)
            give(out, left)

    outs = (near_out, far_out, other_near_out, other_far_out)
    size = start // len(outs)
    for number in range(start // block):

        def give(out, left):
            for first in range(0, block, min(size, block)):
                piece, inside = divmod(number * block + first, size)
                part = min(size, block)
                to = slice(inside, inside + part)
                outs[piece][to, left : left + tile] = out[first : first + part]

        one_block(pl.ds(number * block, block))


def expert_rows(first, pieces, both, down):
    held, width, units = both.shape
    units = units // 2
    rows = sum(p.shape[0] for p in pieces)
    block = min(ROW_BLOCK, rows)
    return pl.pallas_call(
        expert_kernel,
        out_shape=[jax.ShapeDtypeStruct((p.shape[0], width), jnp.bfloat16) for p in pieces],
        in_specs=[SMEM] + [VMEM] * (len(pieces) + 2),
        out_specs=[VMEM] * len(pieces),
        scratch_shapes=[
            pltpu.VMEM((rows, pieces[0].shape[1]), jnp.bfloat16),
            pltpu.VMEM((block, held * units), jnp.bfloat16),
        ],
        compiler_params=pltpu.CompilerParams(vmem_limit_bytes=32 << 20),
        cost_estimate=pl.CostEstimate(
            flops=6 * rows * width * held * units,
            bytes_accessed=4 * rows * width + 6 * held * width * units,
            transcendentals=rows * held * units,
        ),
        name="expert_rows",
    )(first, *pieces, both, down)


def wide(value):
    return value.astype(jnp.float32)


def short(value):
    return value.astype(jnp.bfloat16)


def after(value, *others):
    return lax.optimization_barrier((value, others))[0]


def cut(value, start, size):
    return wide(lax.slice_in_dim(value, start, start + size, axis=0))


class Chunk:
    def __init__(self, rows):
        self.rows = rows
        self.outer = lax.axis_size("ep") // 2
        self.half = rows.shape[0] // 2

    def gather_outer(self, *then):
        rows = after(self.rows, *then)
        ring = [rows] + [turn(rows, step) for step in range(1, self.outer)]
        self.first = jnp.concatenate([r[: self.half] for r in ring], axis=0)
        self.second = jnp.concatenate([r[self.half :] for r in ring], axis=0)

    def gather_near(self, *then):
        first, second = after(self.first, *then), after(self.second, *then)
        self.first = jnp.concatenate([first, flip_inner(first)], axis=0)
        self.second = jnp.concatenate([second, flip_upper(second)], axis=0)

    def gather_far(self):
        self.far_pair = flip_upper(self.first), flip_inner(self.second)

    def gathered_far(self, *then):
        self.pieces = [
            jnp.concatenate([self.first, self.second], axis=0),
            jnp.concatenate(after(self.far_pair, *then), axis=0),
        ]

    def gather_lower(self, *then):
        self.others = [flip_lower(after(p, *then)) for p in self.pieces]

    def back_lower(self):
        self.got = [flip_lower(p) for p in self.away]

    def two(self, number, start, size):
        return cut(self.own[number], start, size) + cut(self.got[number], start, size)

    def back_far(self):
        size = self.own[0].shape[0] // 2
        self.far = short(self.two(1, 0, size)), short(self.two(1, size, size))
        self.far_first, self.far_second = flip_upper(self.far[0]), flip_inner(self.far[1])

    def back_near(self):
        part = self.own[0].shape[0] // 2
        size = part // 2
        first = short(self.two(0, size, size) + cut(self.far_first, size, size))
        second = short(self.two(0, part + size, size) + cut(self.far_second, size, size))
        self.near_first, self.near_second = flip_inner(first), flip_upper(second)

    def block(self, number):
        at, size, part = number * self.half, self.half, self.own[0].shape[0] // 2
        first = self.two(0, at, size) + cut(self.far_first, at, size)
        second = self.two(0, part + at, size) + cut(self.far_second, at, size)
        first = first + cut(self.near_first, at, size)
        second = second + cut(self.near_second, at, size)
        return jnp.concatenate([first, second], axis=0)

    def back_outer(self):
        self.total = self.block(0)
        self.turned = [turn(short(self.block(k)), -k) for k in range(1, self.outer)]

    def finish(self, middle, gain, *then):
        total = middle + self.total
        for turned in after(self.turned, *then):
            total = total + wide(turned)
        return rms_scaled(total, gain).astype(jnp.bfloat16)


def spread(rows):
    size = lax.axis_size("tp")
    both = lax.ppermute(rows, "tp", [(i, i ^ 3) for i in range(size)])
    return [rows, flip_lower(rows), flip_upper(rows), both]


def join_kernel(place_ref, *refs):
    last_ref, out_ref = refs[-2:]
    quarter = out_ref.shape[0] // 4
    size = refs[0].shape[0]
    for number, piece in enumerate(refs[:-2]):
        start = (place_ref[0] ^ number) * quarter
        out_ref[pl.ds(pl.multiple_of(start, size), size), :] = piece[...]
        out_ref[number * quarter + size : (number + 1) * quarter, :] = last_ref[number]


def join(place, pieces, last):
    rows, width = pieces[0].shape
    return pl.pallas_call(
        join_kernel,
        out_shape=jax.ShapeDtypeStruct((rows * 4 * CHUNKS, width), pieces[0].dtype),
        in_specs=[SMEM] + [VMEM] * (len(pieces) + 1),
        out_specs=VMEM,
        compiler_params=pltpu.CompilerParams(vmem_limit_bytes=16 << 20),
        name="join",
    )(place, *pieces, last)


def local(
    resid,
    context,
    w_out,
    pre_gain,
    final_gain,
    w_router,
    expert_ids,
    slot_expert,
    copy_pick,
    w_gate,
    w_up,
    w_down,
):
    held, width, units = w_gate.shape
    row_count = resid.shape[0]
    experts = w_router.shape[1]
    slots = slot_expert.shape[0]
    quarter = row_count // 4
    rows = quarter // CHUNKS
    place = lax.axis_index("tp").astype(jnp.int32).reshape(1)
    first = (lax.axis_index("ep") * held).astype(jnp.int32).reshape(1)
    down = w_down.reshape(held * units, width)

    send, keep = attend(place, context, w_out)
    got = flip_lower(send)
    table = slot_of_pick(after(slot_expert, send), copy_pick, experts)[0]
    lanes = -(-slots // LANES) * LANES
    slot_hot = table[:, None] == jnp.arange(lanes, dtype=jnp.int32)[None, :]
    slot_hot = slot_hot.astype(jnp.bfloat16)

    gain = pre_gain.reshape(1, -1)
    uppers = []
    for number in range(CHUNKS):
        at = slice(number * rows, (number + 1) * rows)
        uppers.append(flip_upper(short(keep[1, at] + wide(got[1, at]))))
    middles, chunks = [], []
    for number in range(CHUNKS):
        middle, row = norm_rows(
            place, keep, got, uppers[number], resid, gain, expert_ids, w_router, slot_hot, number
        )
        middles.append(middle)
        chunks.append(Chunk(row))

    both, down = load_weights(w_gate, w_up, after(down, uppers))

    def serve(chunk, *then):
        pieces = [after(p, *then) for p in chunk.pieces + chunk.others]
        outs = expert_rows(first, pieces, both, down)
        chunk.own, chunk.away = outs[:2], outs[2:]

    one, two = chunks
    one.gather_outer()
    one.gather_near()
    two.gather_outer(one.first)
    one.gather_far()
    two.gather_near()
    one.gathered_far()
    one.gather_lower(one.pieces[1])
    two.gather_far()
    serve(one, two.first, two.second)
    one.back_lower()
    two.gathered_far(one.away)
    two.gather_lower()
    one.back_far()
    serve(two, one.far)
    one.far_first, one.far_second = after((one.far_first, one.far_second), two.away)
    two.back_lower()
    one.back_near()
    two.back_far()
    one.near_first, one.near_second = after((one.near_first, one.near_second), two.far)
    one.back_outer()
    two.back_near()
    two.back_outer()
    result_one = one.finish(middles[0], final_gain)
    ready_one = spread(result_one)
    result_two = two.finish(middles[1], final_gain, result_one)
    return join(place, ready_one, lax.all_gather(result_two, "tp"))


def solution(mesh):
    return jax.shard_map(
        local,
        mesh=mesh,
        in_specs=(
            P("ep", None),
            P("ep", "tp"),
            P("tp", None),
            P(),
            P(),
            P(),
            P("ep", None),
            P(),
            P("ep", None),
            P("ep", None, "tp"),
            P("ep", None, "tp"),
            P("ep", "tp", None),
        ),
        out_specs=P("ep", None),
        check_vma=False,
    )
```

```python
import functools

import jax
import jax.numpy as jnp
from jax import lax
from jax.experimental import pallas as pl
from jax.experimental.pallas import tpu as pltpu
from jax.sharding import PartitionSpec as P

EPSILON = 1e-06
CHUNKS = 2
LANES = 128
ROW_BLOCK = 512


def slot_of_pick(slot_expert, copy_pick, experts):
    count = slot_expert.shape[0]
    order = jnp.arange(count, dtype=jnp.int32)
    same = slot_expert[:, None] == slot_expert[None, :]
    before = order[None, :] < order[:, None]
    rank = jnp.sum((same & before).astype(jnp.int32), axis=1)
    holds = slot_expert[None, :] == jnp.arange(experts, dtype=jnp.int32)[:, None]
    copies = jnp.sum(holds.astype(jnp.int32), axis=1)
    wanted = copy_pick % copies[None, :]
    match = holds[None, :, :] & (rank[None, None, :] == wanted[:, :, None])
    return jnp.sum(match.astype(jnp.int32) * order[None, None, :], axis=2)


def rms_scaled(values, gain):
    mean_square = jnp.mean(values * values, axis=-1, keepdims=True)
    return values * lax.rsqrt(mean_square + EPSILON) * gain.astype(jnp.float32)


def turn(value, step):
    count = lax.axis_size("ep")
    return lax.ppermute(value, "ep", [(i, (i + 2 * step) % count) for i in range(count)])


def flip_inner(value):
    return lax.ppermute(value, "ep", [(i, i ^ 1) for i in range(lax.axis_size("ep"))])


def flip_upper(value):
    return lax.ppermute(value, "tp", [(i, i ^ 2) for i in range(lax.axis_size("tp"))])


def flip_lower(value):
    return lax.ppermute(value, "tp", [(i, i ^ 1) for i in range(lax.axis_size("tp"))])


VMEM = pl.BlockSpec(memory_space=pltpu.VMEM)
SMEM = pl.BlockSpec(memory_space=pltpu.SMEM)
ANY = pl.BlockSpec(memory_space=pl.ANY)


def attend_kernel(place_ref, first_ref, context_ref, w_ref, send_ref, keep_ref):
    place = place_ref[0]
    quarter = send_ref.shape[1]
    rows = []
    for lower in (1, 0):
        for upper in (0, 1):
            start = pl.multiple_of((place ^ (upper * 2 + lower)) * quarter, quarter)
            rows.append(context_ref[pl.ds(start, quarter), :])
    rows = jnp.concatenate(rows, axis=0)
    width = w_ref.shape[1]
    tile = 512 if width % 512 == 0 else width
    for left in range(0, width, tile):
        out = jnp.dot(rows, w_ref[:, left : left + tile], preferred_element_type=jnp.float32)
        for upper in (0, 1):
            send_ref[upper, :, left : left + tile] = out[
                upper * quarter : (upper + 1) * quarter
            ].astype(jnp.bfloat16)
            keep_ref[upper, :, left : left + tile] = out[
                (upper + 2) * quarter : (upper + 3) * quarter
            ]


def attend(place, first, context, w_out):
    rows, _ = context.shape
    width = w_out.shape[1]
    quarter = rows // 4
    return pl.pallas_call(
        attend_kernel,
        out_shape=(
            jax.ShapeDtypeStruct((2, quarter, width), jnp.bfloat16),
            jax.ShapeDtypeStruct((2, quarter, width), jnp.float32),
        ),
        in_specs=[SMEM, SMEM, VMEM, VMEM],
        out_specs=(VMEM, VMEM),
        compiler_params=pltpu.CompilerParams(vmem_limit_bytes=16 << 20),
        name="attend",
    )(place, first, context, w_out)


def norm_kernel(
    place_ref,
    keep_ref,
    lower_ref,
    upper_ref,
    resid_ref,
    gain_ref,
    ids_ref,
    router_ref,
    slot_hot_ref,
    middle_ref,
    row_ref,
):
    attention = (
        keep_ref[0] + lower_ref[0].astype(jnp.float32) + upper_ref[...].astype(jnp.float32)
    )
    middle = resid_ref[...].astype(jnp.float32) + attention
    middle_ref[...] = middle
    width = middle.shape[1]
    normed = rms_scaled(middle, gain_ref[...]).astype(jnp.bfloat16)
    row_ref[:, :width] = normed
    logits = jnp.dot(normed, router_ref[...], preferred_element_type=jnp.float32)
    expert = lax.broadcasted_iota(jnp.int32, logits.shape, 1)
    ids = ids_ref[...]
    hit = ids[:, 0:1] == expert
    for choice in range(1, ids.shape[1]):
        hit = hit | (ids[:, choice : choice + 1] == expert)
    raised = jnp.where(hit, jnp.exp(logits), 0.0)
    weights = (raised / jnp.sum(raised, axis=1, keepdims=True)).astype(jnp.bfloat16)
    row_ref[:, width:] = jnp.dot(
        weights, slot_hot_ref[...], preferred_element_type=jnp.float32
    ).astype(jnp.bfloat16)


def norm_rows(place, keep, from_lower, from_upper, resid, gain, ids, router, slot_hot, number):
    rows, width = from_upper.shape
    chunks = keep.shape[1] // rows
    extra = slot_hot.shape[1]

    def whole(array):
        return pl.BlockSpec(array.shape, lambda i, p: (0, 0))

    def mine(array):
        return pl.BlockSpec((rows, array.shape[1]), lambda i, p: (p[0] * chunks + number, 0))

    return pl.pallas_call(
        norm_kernel,
        out_shape=(
            jax.ShapeDtypeStruct((rows, width), jnp.float32),
            jax.ShapeDtypeStruct((rows, width + extra), jnp.bfloat16),
        ),
        grid_spec=pltpu.PrefetchScalarGridSpec(
            num_scalar_prefetch=1,
            grid=(1,),
            in_specs=[
                pl.BlockSpec((1, rows, width), lambda i, p: (0, number, 0)),
                pl.BlockSpec((1, rows, width), lambda i, p: (0, number, 0)),
                whole(from_upper),
                mine(resid),
                whole(gain),
                mine(ids),
                whole(router),
                whole(slot_hot),
            ],
            out_specs=[
                pl.BlockSpec((rows, width), lambda i, p: (0, 0)),
                pl.BlockSpec((rows, width + extra), lambda i, p: (0, 0)),
            ],
        ),
        compiler_params=pltpu.CompilerParams(vmem_limit_bytes=16 << 20),
        name="norm_rows",
    )(place, keep, from_lower, from_upper, resid, gain, ids, router, slot_hot)


def load_kernel(gate_hbm, up_hbm, down_hbm, both_ref, down_ref, mark_ref, sems):
    units = gate_hbm.shape[2]
    copies = [
        pltpu.make_async_copy(gate_hbm, both_ref.at[:, :, pl.ds(0, units)], sems.at[0]),
        pltpu.make_async_copy(up_hbm, both_ref.at[:, :, pl.ds(units, units)], sems.at[1]),
        pltpu.make_async_copy(down_hbm, down_ref, sems.at[2]),
    ]
    for copy in copies:
        copy.start()
    mark_ref[...] = jnp.zeros_like(mark_ref)
    for copy in copies:
        copy.wait()


def load_weights(w_gate, w_up, w_down):
    held, width, units = w_gate.shape
    return pl.pallas_call(
        load_kernel,
        out_shape=(
            pltpu.VMEM((held, width, 2 * units), jnp.bfloat16),
            pltpu.VMEM((held * units, width), jnp.bfloat16),
            jax.ShapeDtypeStruct((8, LANES), jnp.int32),
        ),
        in_specs=[ANY] * 3,
        out_specs=(VMEM, VMEM, VMEM),
        scratch_shapes=[pltpu.SemaphoreType.DMA((3,))],
        compiler_params=pltpu.CompilerParams(vmem_limit_bytes=2 << 20),
        name="load_weights",
    )(w_gate, w_up, w_down)


def expert_kernel(
    first_ref,
    near_ref,
    far_ref,
    other_near_ref,
    other_far_ref,
    both_ref,
    down_ref,
    loaded_hbm,
    near_out,
    far_out,
    other_near_out,
    other_far_out,
    rows_ref,
    hidden_ref,
):
    held, width, units = both_ref.shape
    units = units // 2
    start = 0
    for piece in (near_ref, far_ref, other_near_ref, other_far_ref):
        rows_ref[start : start + piece.shape[0]] = piece[...]
        start += piece.shape[0]
    block = min(ROW_BLOCK, start)
    extra = rows_ref.shape[1] - width
    mine = lax.broadcasted_iota(jnp.int32, (extra, LANES), 1) + first_ref[0]
    mine = (lax.broadcasted_iota(jnp.int32, (extra, LANES), 0) == mine).astype(jnp.bfloat16)
    tile = 512 if width % 512 == 0 else width

    def one_block(at):
        weights = jnp.dot(rows_ref[at, width:], mine, preferred_element_type=jnp.float32)
        for slot in range(held):
            out = jnp.dot(rows_ref[at, :width], both_ref[slot], preferred_element_type=jnp.float32)
            gate, upper = out[:, :units], out[:, units:]
            hidden = jax.nn.silu(gate) * upper * weights[:, slot : slot + 1]
            hidden_ref[:, slot * units : (slot + 1) * units] = hidden.astype(jnp.bfloat16)
        for left in range(0, width, tile):
            out = jnp.dot(
                hidden_ref[...],
                down_ref[:, left : left + tile],
                preferred_element_type=jnp.float32,
            ).astype(jnp.bfloat16)
            give(out, left)

    outs = (near_out, far_out, other_near_out, other_far_out)
    size = start // len(outs)
    for number in range(start // block):

        def give(out, left):
            for first in range(0, block, min(size, block)):
                piece, inside = divmod(number * block + first, size)
                part = min(size, block)
                to = slice(inside, inside + part)
                outs[piece][to, left : left + tile] = out[first : first + part]

        one_block(pl.ds(number * block, block))


def expert_rows(first, pieces, both, down, loaded):
    held, width, units = both.shape
    units = units // 2
    rows = sum(p.shape[0] for p in pieces)
    block = min(ROW_BLOCK, rows)
    return pl.pallas_call(
        expert_kernel,
        out_shape=[jax.ShapeDtypeStruct((p.shape[0], width), jnp.bfloat16) for p in pieces],
        in_specs=[SMEM] + [VMEM] * (len(pieces) + 2) + [ANY],
        out_specs=[VMEM] * len(pieces),
        scratch_shapes=[
            pltpu.VMEM((rows, pieces[0].shape[1]), jnp.bfloat16),
            pltpu.VMEM((block, held * units), jnp.bfloat16),
        ],
        compiler_params=pltpu.CompilerParams(vmem_limit_bytes=32 << 20),
        cost_estimate=pl.CostEstimate(
            flops=6 * rows * width * held * units,
            bytes_accessed=4 * rows * width + 6 * held * width * units,
            transcendentals=rows * held * units,
        ),
        name="expert_rows",
    )(first, *pieces, both, down, loaded)


def wide(value):
    return value.astype(jnp.float32)


def short(value):
    return value.astype(jnp.bfloat16)


def after(value, *others):
    return lax.optimization_barrier((value, others))[0]


def cut(value, start, size):
    return wide(lax.slice_in_dim(value, start, start + size, axis=0))


class Chunk:
    def __init__(self, rows):
        self.rows = rows
        self.outer = lax.axis_size("ep") // 2
        self.half = rows.shape[0] // 2

    def gather_outer(self, *then):
        rows = after(self.rows, *then)
        ring = [rows] + [turn(rows, step) for step in range(1, self.outer)]
        self.first = jnp.concatenate([r[: self.half] for r in ring], axis=0)
        self.second = jnp.concatenate([r[self.half :] for r in ring], axis=0)

    def gather_near(self, *then):
        first, second = after(self.first, *then), after(self.second, *then)
        self.first = jnp.concatenate([first, flip_inner(first)], axis=0)
        self.second = jnp.concatenate([second, flip_upper(second)], axis=0)

    def gather_far(self):
        self.far_pair = flip_upper(self.first), flip_inner(self.second)

    def gathered_far(self, *then):
        self.pieces = [
            jnp.concatenate([self.first, self.second], axis=0),
            jnp.concatenate(after(self.far_pair, *then), axis=0),
        ]

    def gather_lower(self, *then):
        self.others = [flip_lower(after(p, *then)) for p in self.pieces]

    def back_lower(self):
        self.got = [flip_lower(p) for p in self.away]

    def two(self, number, start, size):
        return cut(self.own[number], start, size) + cut(self.got[number], start, size)

    def back_far(self):
        size = self.own[0].shape[0] // 2
        self.far = short(self.two(1, 0, size)), short(self.two(1, size, size))
        self.far_first, self.far_second = flip_upper(self.far[0]), flip_inner(self.far[1])

    def back_near(self):
        part = self.own[0].shape[0] // 2
        size = part // 2
        first = short(self.two(0, size, size) + cut(self.far_first, size, size))
        second = short(self.two(0, part + size, size) + cut(self.far_second, size, size))
        self.near = first, second
        self.near_first, self.near_second = flip_inner(first), flip_upper(second)

    def block(self, number):
        at, size, part = number * self.half, self.half, self.own[0].shape[0] // 2
        first = self.two(0, at, size) + cut(self.far_first, at, size)
        second = self.two(0, part + at, size) + cut(self.far_second, at, size)
        first = first + cut(self.near_first, at, size)
        second = second + cut(self.near_second, at, size)
        return jnp.concatenate([first, second], axis=0)

    def back_outer(self):
        self.total = self.block(0)
        self.turned = [turn(short(self.block(k)), -k) for k in range(1, self.outer)]

    def finish(self, middle, gain, *then):
        total = middle + self.total
        for turned in after(self.turned, *then):
            total = total + wide(turned)
        return rms_scaled(total, gain).astype(jnp.bfloat16)


def spread(rows):
    size = lax.axis_size("tp")
    both = lax.ppermute(rows, "tp", [(i, i ^ 3) for i in range(size)])
    return [rows, flip_lower(rows), flip_upper(rows), both]


def join_kernel(place_ref, *refs):
    last_ref, out_ref = refs[-2:]
    quarter = out_ref.shape[0] // 4
    size = refs[0].shape[0]
    for number, piece in enumerate(refs[:-2]):
        start = (place_ref[0] ^ number) * quarter
        out_ref[pl.ds(pl.multiple_of(start, size), size), :] = piece[...]
        out_ref[number * quarter + size : (number + 1) * quarter, :] = last_ref[number]


def join(place, pieces, last):
    rows, width = pieces[0].shape
    return pl.pallas_call(
        join_kernel,
        out_shape=jax.ShapeDtypeStruct((rows * 4 * CHUNKS, width), pieces[0].dtype),
        in_specs=[SMEM] + [VMEM] * (len(pieces) + 1),
        out_specs=VMEM,
        compiler_params=pltpu.CompilerParams(vmem_limit_bytes=16 << 20),
        name="join",
    )(place, *pieces, last)


def local(
    resid,
    context,
    w_out,
    pre_gain,
    final_gain,
    w_router,
    expert_ids,
    slot_expert,
    copy_pick,
    w_gate,
    w_up,
    w_down,
):
    held, width, units = w_gate.shape
    row_count = resid.shape[0]
    experts = w_router.shape[1]
    slots = slot_expert.shape[0]
    quarter = row_count // 4
    rows = quarter // CHUNKS
    place = lax.axis_index("tp").astype(jnp.int32).reshape(1)
    first = (lax.axis_index("ep") * held).astype(jnp.int32).reshape(1)
    down = w_down.reshape(held * units, width)

    send, keep = attend(place, first, context, w_out)
    got = flip_lower(send)
    table = slot_of_pick(after(slot_expert, send), copy_pick, experts)[0]
    lanes = -(-slots // LANES) * LANES
    slot_hot = table[:, None] == jnp.arange(lanes, dtype=jnp.int32)[None, :]
    slot_hot = slot_hot.astype(jnp.bfloat16)

    gain = pre_gain.reshape(1, -1)
    uppers = []
    for number in range(CHUNKS):
        at = slice(number * rows, (number + 1) * rows)
        uppers.append(flip_upper(short(keep[1, at] + wide(got[1, at]))))
    middles, chunks = [], []
    for number in range(CHUNKS):
        middle, row = norm_rows(
            place, keep, got, uppers[number], resid, gain, expert_ids, w_router, slot_hot, number
        )
        middles.append(middle)
        chunks.append(Chunk(row))

    both, down, loaded = load_weights(w_gate, w_up, after(down, uppers))

    def serve(chunk, *then):
        pieces = [after(p, *then) for p in chunk.pieces + chunk.others]
        outs = expert_rows(first, pieces, both, down, loaded)
        chunk.own, chunk.away = outs[:2], outs[2:]

    one, two = chunks
    one.gather_outer()
    one.first, one.second = after((one.first, one.second), loaded)
    two.gather_outer(one.first)
    one.gather_near()
    one.gather_far()
    two.gather_near()
    one.gathered_far(two.first, two.second)
    one.gather_lower(one.pieces[1])
    two.gather_far()
    serve(one)
    one.back_lower()
    two.gathered_far(one.away)
    two.gather_lower()
    one.back_far()
    serve(two, one.far)
    one.far_first, one.far_second = after((one.far_first, one.far_second), two.away)
    two.back_lower()
    one.back_near()
    two.back_far()
    one.near_first, one.near_second = after((one.near_first, one.near_second), two.far)
    one.back_outer()
    two.back_near()
    two.back_outer()
    result_one = one.finish(middles[0], final_gain, two.near)
    ready_one = spread(result_one)
    result_two = two.finish(middles[1], final_gain, result_one)
    return join(place, ready_one, lax.all_gather(result_two, "tp"))


def solution(mesh):
    return jax.shard_map(
        local,
        mesh=mesh,
        in_specs=(
            P("ep", None),
            P("ep", "tp"),
            P("tp", None),
            P(),
            P(),
            P(),
            P("ep", None),
            P(),
            P("ep", None),
            P("ep", None, "tp"),
            P("ep", None, "tp"),
            P("ep", "tp", None),
        ),
        out_specs=P("ep", None),
        check_vma=False,
    )
```

```python
import functools

import jax
import jax.numpy as jnp
from jax import lax
from jax.experimental import pallas as pl
from jax.experimental.pallas import tpu as pltpu
from jax.sharding import PartitionSpec as P

EPSILON = 1e-06
CHUNKS = 2
LANES = 128
ROW_BLOCK = 512


def slot_of_pick(slot_expert, copy_pick, experts):
    count = slot_expert.shape[0]
    order = jnp.arange(count, dtype=jnp.int32)
    same = slot_expert[:, None] == slot_expert[None, :]
    before = order[None, :] < order[:, None]
    rank = jnp.sum((same & before).astype(jnp.int32), axis=1)
    holds = slot_expert[None, :] == jnp.arange(experts, dtype=jnp.int32)[:, None]
    copies = jnp.sum(holds.astype(jnp.int32), axis=1)
    wanted = copy_pick % copies[None, :]
    match = holds[None, :, :] & (rank[None, None, :] == wanted[:, :, None])
    return jnp.sum(match.astype(jnp.int32) * order[None, None, :], axis=2)


def rms_scaled(values, gain):
    mean_square = jnp.mean(values * values, axis=-1, keepdims=True)
    return values * lax.rsqrt(mean_square + EPSILON) * gain.astype(jnp.float32)


def turn(value, step):
    count = lax.axis_size("ep")
    return lax.ppermute(value, "ep", [(i, (i + 2 * step) % count) for i in range(count)])


def flip_inner(value):
    return lax.ppermute(value, "ep", [(i, i ^ 1) for i in range(lax.axis_size("ep"))])


def flip_upper(value):
    return lax.ppermute(value, "tp", [(i, i ^ 2) for i in range(lax.axis_size("tp"))])


def flip_lower(value):
    return lax.ppermute(value, "tp", [(i, i ^ 1) for i in range(lax.axis_size("tp"))])


VMEM = pl.BlockSpec(memory_space=pltpu.VMEM)
SMEM = pl.BlockSpec(memory_space=pltpu.SMEM)
ANY = pl.BlockSpec(memory_space=pl.ANY)


def attend_kernel(place_ref, first_ref, context_ref, w_ref, send_ref, keep_ref):
    place = place_ref[0]
    quarter = send_ref.shape[1]
    rows = []
    for lower in (1, 0):
        for upper in (0, 1):
            start = pl.multiple_of((place ^ (upper * 2 + lower)) * quarter, quarter)
            rows.append(context_ref[pl.ds(start, quarter), :])
    rows = jnp.concatenate(rows, axis=0)
    width = w_ref.shape[1]
    tile = 512 if width % 512 == 0 else width
    for left in range(0, width, tile):
        out = jnp.dot(rows, w_ref[:, left : left + tile], preferred_element_type=jnp.float32)
        for upper in (0, 1):
            send_ref[upper, :, left : left + tile] = out[
                upper * quarter : (upper + 1) * quarter
            ].astype(jnp.bfloat16)
            keep_ref[upper, :, left : left + tile] = out[
                (upper + 2) * quarter : (upper + 3) * quarter
            ]


def attend(place, first, context, w_out):
    rows, _ = context.shape
    width = w_out.shape[1]
    quarter = rows // 4
    return pl.pallas_call(
        attend_kernel,
        out_shape=(
            jax.ShapeDtypeStruct((2, quarter, width), jnp.bfloat16),
            jax.ShapeDtypeStruct((2, quarter, width), jnp.float32),
        ),
        in_specs=[SMEM, SMEM, VMEM, VMEM],
        out_specs=(VMEM, VMEM),
        compiler_params=pltpu.CompilerParams(vmem_limit_bytes=16 << 20),
        name="attend",
    )(place, first, context, w_out)


def norm_kernel(
    place_ref,
    keep_ref,
    lower_ref,
    upper_ref,
    resid_ref,
    gain_ref,
    ids_ref,
    router_ref,
    slot_hot_ref,
    middle_ref,
    row_ref,
):
    attention = (
        keep_ref[0] + lower_ref[0].astype(jnp.float32) + upper_ref[...].astype(jnp.float32)
    )
    middle = resid_ref[...].astype(jnp.float32) + attention
    middle_ref[...] = middle
    width = middle.shape[1]
    normed = rms_scaled(middle, gain_ref[...]).astype(jnp.bfloat16)
    row_ref[:, :width] = normed
    logits = jnp.dot(normed, router_ref[...], preferred_element_type=jnp.float32)
    expert = lax.broadcasted_iota(jnp.int32, logits.shape, 1)
    ids = ids_ref[...]
    hit = ids[:, 0:1] == expert
    for choice in range(1, ids.shape[1]):
        hit = hit | (ids[:, choice : choice + 1] == expert)
    raised = jnp.where(hit, jnp.exp(logits), 0.0)
    weights = (raised / jnp.sum(raised, axis=1, keepdims=True)).astype(jnp.bfloat16)
    row_ref[:, width:] = jnp.dot(
        weights, slot_hot_ref[...], preferred_element_type=jnp.float32
    ).astype(jnp.bfloat16)


def norm_rows(place, keep, from_lower, from_upper, resid, gain, ids, router, slot_hot, number):
    rows, width = from_upper.shape
    chunks = keep.shape[1] // rows
    extra = slot_hot.shape[1]

    def whole(array):
        return pl.BlockSpec(array.shape, lambda i, p: (0, 0))

    def mine(array):
        return pl.BlockSpec((rows, array.shape[1]), lambda i, p: (p[0] * chunks + number, 0))

    return pl.pallas_call(
        norm_kernel,
        out_shape=(
            jax.ShapeDtypeStruct((rows, width), jnp.float32),
            jax.ShapeDtypeStruct((rows, width + extra), jnp.bfloat16),
        ),
        grid_spec=pltpu.PrefetchScalarGridSpec(
            num_scalar_prefetch=1,
            grid=(1,),
            in_specs=[
                pl.BlockSpec((1, rows, width), lambda i, p: (0, number, 0)),
                pl.BlockSpec((1, rows, width), lambda i, p: (0, number, 0)),
                whole(from_upper),
                mine(resid),
                whole(gain),
                mine(ids),
                whole(router),
                whole(slot_hot),
            ],
            out_specs=[
                pl.BlockSpec((rows, width), lambda i, p: (0, 0)),
                pl.BlockSpec((rows, width + extra), lambda i, p: (0, 0)),
            ],
        ),
        compiler_params=pltpu.CompilerParams(vmem_limit_bytes=16 << 20),
        name="norm_rows",
    )(place, keep, from_lower, from_upper, resid, gain, ids, router, slot_hot)


def load_kernel(gate_hbm, up_hbm, down_hbm, both_ref, down_ref, mark_ref, sems):
    units = gate_hbm.shape[2]
    copies = [
        pltpu.make_async_copy(gate_hbm, both_ref.at[:, :, pl.ds(0, units)], sems.at[0]),
        pltpu.make_async_copy(up_hbm, both_ref.at[:, :, pl.ds(units, units)], sems.at[1]),
        pltpu.make_async_copy(down_hbm, down_ref, sems.at[2]),
    ]
    for copy in copies:
        copy.start()
    mark_ref[...] = jnp.zeros_like(mark_ref)
    for copy in copies:
        copy.wait()


def load_weights(w_gate, w_up, w_down):
    held, width, units = w_gate.shape
    return pl.pallas_call(
        load_kernel,
        out_shape=(
            pltpu.VMEM((held, width, 2 * units), jnp.bfloat16),
            pltpu.VMEM((held * units, width), jnp.bfloat16),
            jax.ShapeDtypeStruct((8, LANES), jnp.int32),
        ),
        in_specs=[ANY] * 3,
        out_specs=(VMEM, VMEM, VMEM),
        scratch_shapes=[pltpu.SemaphoreType.DMA((3,))],
        compiler_params=pltpu.CompilerParams(vmem_limit_bytes=2 << 20),
        name="load_weights",
    )(w_gate, w_up, w_down)


def expert_kernel(
    first_ref,
    near_ref,
    far_ref,
    both_ref,
    down_ref,
    loaded_hbm,
    near_out,
    far_out,
    rows_ref,
    hidden_ref,
):
    held, width, units = both_ref.shape
    units = units // 2
    start = 0
    for piece in (near_ref, far_ref):
        rows_ref[start : start + piece.shape[0]] = piece[...]
        start += piece.shape[0]
    block = min(ROW_BLOCK, start)
    extra = rows_ref.shape[1] - width
    mine = lax.broadcasted_iota(jnp.int32, (extra, LANES), 1) + first_ref[0]
    mine = (lax.broadcasted_iota(jnp.int32, (extra, LANES), 0) == mine).astype(jnp.bfloat16)
    tile = 512 if width % 512 == 0 else width

    def one_block(at):
        weights = jnp.dot(rows_ref[at, width:], mine, preferred_element_type=jnp.float32)
        for slot in range(held):
            out = jnp.dot(rows_ref[at, :width], both_ref[slot], preferred_element_type=jnp.float32)
            gate, upper = out[:, :units], out[:, units:]
            hidden = jax.nn.silu(gate) * upper * weights[:, slot : slot + 1]
            hidden_ref[:, slot * units : (slot + 1) * units] = hidden.astype(jnp.bfloat16)
        for left in range(0, width, tile):
            out = jnp.dot(
                hidden_ref[...],
                down_ref[:, left : left + tile],
                preferred_element_type=jnp.float32,
            ).astype(jnp.bfloat16)
            give(out, left)

    outs = (near_out, far_out)
    size = start // len(outs)
    for number in range(start // block):

        def give(out, left):
            for first in range(0, block, min(size, block)):
                piece, inside = divmod(number * block + first, size)
                part = min(size, block)
                to = slice(inside, inside + part)
                outs[piece][to, left : left + tile] = out[first : first + part]

        one_block(pl.ds(number * block, block))


def expert_rows(first, pieces, both, down, loaded):
    held, width, units = both.shape
    units = units // 2
    rows = sum(p.shape[0] for p in pieces)
    block = min(ROW_BLOCK, rows)
    return pl.pallas_call(
        expert_kernel,
        out_shape=[jax.ShapeDtypeStruct((p.shape[0], width), jnp.bfloat16) for p in pieces],
        in_specs=[SMEM] + [VMEM] * (len(pieces) + 2) + [ANY],
        out_specs=[VMEM] * len(pieces),
        scratch_shapes=[
            pltpu.VMEM((rows, pieces[0].shape[1]), jnp.bfloat16),
            pltpu.VMEM((block, held * units), jnp.bfloat16),
        ],
        compiler_params=pltpu.CompilerParams(vmem_limit_bytes=32 << 20),
        cost_estimate=pl.CostEstimate(
            flops=6 * rows * width * held * units,
            bytes_accessed=4 * rows * width + 6 * held * width * units,
            transcendentals=rows * held * units,
        ),
        name="expert_rows",
    )(first, *pieces, both, down, loaded)


def wide(value):
    return value.astype(jnp.float32)


def short(value):
    return value.astype(jnp.bfloat16)


def after(value, *others):
    return lax.optimization_barrier((value, others))[0]


def cut(value, start, size):
    return wide(lax.slice_in_dim(value, start, start + size, axis=0))


class Chunk:
    def __init__(self, rows):
        self.rows = rows
        self.outer = lax.axis_size("ep") // 2
        self.half = rows.shape[0] // 2

    def gather_outer(self, *then):
        rows = after(self.rows, *then)
        ring = [rows] + [turn(rows, step) for step in range(1, self.outer)]
        self.first = jnp.concatenate([r[: self.half] for r in ring], axis=0)
        self.second = jnp.concatenate([r[self.half :] for r in ring], axis=0)

    def gather_near(self, *then):
        first, second = after(self.first, *then), after(self.second, *then)
        inner, upper = lax.optimization_barrier((flip_inner(first), flip_upper(second)))
        self.first = jnp.concatenate([first, inner], axis=0)
        self.second = jnp.concatenate([second, upper], axis=0)

    def gather_far(self):
        self.far_pair = flip_upper(self.first), flip_inner(self.second)

    def gathered_far(self, *then):
        self.pieces = [
            jnp.concatenate([self.first, self.second], axis=0),
            jnp.concatenate(after(self.far_pair, *then), axis=0),
        ]

    def gather_lower(self, *then):
        self.others = [flip_lower(after(p, *then)) for p in self.pieces]

    def back_lower(self):
        self.got = [flip_lower(p) for p in self.away]

    def two(self, number, start, size):
        return cut(self.own[number], start, size) + cut(self.got[number], start, size)

    def back_far(self):
        size = self.own[0].shape[0] // 2
        self.far = short(self.two(1, 0, size)), short(self.two(1, size, size))
        self.far_first, self.far_second = flip_upper(self.far[0]), flip_inner(self.far[1])

    def back_near(self):
        part = self.own[0].shape[0] // 2
        size = part // 2
        first = short(self.two(0, size, size) + cut(self.far_first, size, size))
        second = short(self.two(0, part + size, size) + cut(self.far_second, size, size))
        self.near = first, second
        self.near_first, self.near_second = flip_inner(first), flip_upper(second)

    def block(self, number):
        at, size, part = number * self.half, self.half, self.own[0].shape[0] // 2
        first = self.two(0, at, size) + cut(self.far_first, at, size)
        second = self.two(0, part + at, size) + cut(self.far_second, at, size)
        first = first + cut(self.near_first, at, size)
        second = second + cut(self.near_second, at, size)
        return jnp.concatenate([first, second], axis=0)

    def back_outer(self):
        self.total = self.block(0)
        self.turned = [turn(short(self.block(k)), -k) for k in range(1, self.outer)]

    def finish(self, middle, gain, *then):
        total = middle + self.total
        for turned in after(self.turned, *then):
            total = total + wide(turned)
        return rms_scaled(total, gain).astype(jnp.bfloat16)


def spread(rows):
    size = lax.axis_size("tp")
    both = lax.ppermute(rows, "tp", [(i, i ^ 3) for i in range(size)])
    return [rows, flip_lower(rows), flip_upper(rows), both]


def join_kernel(place_ref, *refs):
    last_ref, out_ref = refs[-2:]
    quarter = out_ref.shape[0] // 4
    size = refs[0].shape[0]
    for number, piece in enumerate(refs[:-2]):
        start = (place_ref[0] ^ number) * quarter
        out_ref[pl.ds(pl.multiple_of(start, size), size), :] = piece[...]
        out_ref[number * quarter + size : (number + 1) * quarter, :] = last_ref[number]


def join(place, pieces, last):
    rows, width = pieces[0].shape
    return pl.pallas_call(
        join_kernel,
        out_shape=jax.ShapeDtypeStruct((rows * 4 * CHUNKS, width), pieces[0].dtype),
        in_specs=[SMEM] + [VMEM] * (len(pieces) + 1),
        out_specs=VMEM,
        compiler_params=pltpu.CompilerParams(vmem_limit_bytes=16 << 20),
        name="join",
    )(place, *pieces, last)


def local(
    resid,
    context,
    w_out,
    pre_gain,
    final_gain,
    w_router,
    expert_ids,
    slot_expert,
    copy_pick,
    w_gate,
    w_up,
    w_down,
):
    held, width, units = w_gate.shape
    row_count = resid.shape[0]
    experts = w_router.shape[1]
    slots = slot_expert.shape[0]
    quarter = row_count // 4
    rows = quarter // CHUNKS
    place = lax.axis_index("tp").astype(jnp.int32).reshape(1)
    first = (lax.axis_index("ep") * held).astype(jnp.int32).reshape(1)
    down = w_down.reshape(held * units, width)

    send, keep = attend(place, first, context, w_out)
    got = flip_lower(send)
    parts = []
    for number in range(CHUNKS):
        at = slice(number * rows, (number + 1) * rows)
        parts.append(short(keep[1, at] + wide(got[1, at])))
    table = slot_of_pick(after(slot_expert, parts[0]), copy_pick, experts)[0]
    lanes = -(-slots // LANES) * LANES
    slot_hot = table[:, None] == jnp.arange(lanes, dtype=jnp.int32)[None, :]
    slot_hot = slot_hot.astype(jnp.bfloat16)

    gain = pre_gain.reshape(1, -1)
    uppers = [flip_upper(part) for part in parts]
    middles, chunks = [], []
    for number in range(CHUNKS):
        middle, row = norm_rows(
            place, keep, got, uppers[number], resid, gain, expert_ids, w_router, slot_hot, number
        )
        middles.append(middle)
        chunks.append(Chunk(row))

    both, down, loaded = load_weights(w_gate, w_up, after(down, uppers))

    def serve(pieces, *then):
        return expert_rows(first, [after(p, *then) for p in pieces], both, down, loaded)

    one, two = chunks
    one.gather_outer()
    one.first, one.second = after((one.first, one.second), loaded)
    one.gather_near()
    two.gather_outer(one.first)
    one.gather_far()
    two.gather_near()
    one.gathered_far()
    one.gather_lower(one.pieces[1])
    two.gather_far()
    one.away = serve(one.others)
    one.back_lower()
    one.own = serve(one.pieces, one.away)
    two.gathered_far(one.own)
    two.gather_lower()
    one.back_far()
    two.away = serve(two.others, one.far)
    two.back_lower()
    two.own = serve(two.pieces, two.away)
    one.far_first, one.far_second = after((one.far_first, one.far_second), two.own)
    one.back_near()
    two.back_far()
    one.near_first, one.near_second = after((one.near_first, one.near_second), two.far)
    one.back_outer()
    two.back_near()
    two.back_outer()
    result_one = one.finish(middles[0], final_gain, two.near)
    ready_one = spread(result_one)
    result_two = two.finish(middles[1], final_gain, result_one)
    return join(place, ready_one, lax.all_gather(result_two, "tp"))


def solution(mesh):
    return jax.shard_map(
        local,
        mesh=mesh,
        in_specs=(
            P("ep", None),
            P("ep", "tp"),
            P("tp", None),
            P(),
            P(),
            P(),
            P("ep", None),
            P(),
            P("ep", None),
            P("ep", None, "tp"),
            P("ep", None, "tp"),
            P("ep", "tp", None),
        ),
        out_specs=P("ep", None),
        check_vma=False,
    )
```

```python
import functools

import jax
import jax.numpy as jnp
from jax import lax
from jax.experimental import pallas as pl
from jax.experimental.pallas import tpu as pltpu
from jax.sharding import PartitionSpec as P

EPSILON = 1e-06
CHUNKS = 2
LANES = 128
ROW_BLOCK = 512


def slot_of_pick(slot_expert, copy_pick, experts):
    count = slot_expert.shape[0]
    order = jnp.arange(count, dtype=jnp.int32)
    same = slot_expert[:, None] == slot_expert[None, :]
    before = order[None, :] < order[:, None]
    rank = jnp.sum((same & before).astype(jnp.int32), axis=1)
    holds = slot_expert[None, :] == jnp.arange(experts, dtype=jnp.int32)[:, None]
    copies = jnp.sum(holds.astype(jnp.int32), axis=1)
    wanted = copy_pick % copies[None, :]
    match = holds[None, :, :] & (rank[None, None, :] == wanted[:, :, None])
    return jnp.sum(match.astype(jnp.int32) * order[None, None, :], axis=2)


def rms_scaled(values, gain):
    mean_square = jnp.mean(values * values, axis=-1, keepdims=True)
    return values * lax.rsqrt(mean_square + EPSILON) * gain.astype(jnp.float32)


def turn(value, step):
    count = lax.axis_size("ep")
    return lax.ppermute(value, "ep", [(i, (i + 2 * step) % count) for i in range(count)])


def flip_inner(value):
    return lax.ppermute(value, "ep", [(i, i ^ 1) for i in range(lax.axis_size("ep"))])


def flip_upper(value):
    return lax.ppermute(value, "tp", [(i, i ^ 2) for i in range(lax.axis_size("tp"))])


def flip_lower(value):
    return lax.ppermute(value, "tp", [(i, i ^ 1) for i in range(lax.axis_size("tp"))])


VMEM = pl.BlockSpec(memory_space=pltpu.VMEM)
SMEM = pl.BlockSpec(memory_space=pltpu.SMEM)
ANY = pl.BlockSpec(memory_space=pl.ANY)


def attend_kernel(place_ref, first_ref, context_ref, w_ref, send_ref, keep_ref):
    place = place_ref[0]
    quarter = send_ref.shape[1]
    rows = []
    for lower in (1, 0):
        for upper in (0, 1):
            start = pl.multiple_of((place ^ (upper * 2 + lower)) * quarter, quarter)
            rows.append(context_ref[pl.ds(start, quarter), :])
    rows = jnp.concatenate(rows, axis=0)
    width = w_ref.shape[1]
    tile = 512 if width % 512 == 0 else width
    for left in range(0, width, tile):
        out = jnp.dot(rows, w_ref[:, left : left + tile], preferred_element_type=jnp.float32)
        for upper in (0, 1):
            send_ref[upper, :, left : left + tile] = out[
                upper * quarter : (upper + 1) * quarter
            ].astype(jnp.bfloat16)
            keep_ref[upper, :, left : left + tile] = out[
                (upper + 2) * quarter : (upper + 3) * quarter
            ]


def attend(place, first, context, w_out):
    rows, _ = context.shape
    width = w_out.shape[1]
    quarter = rows // 4
    return pl.pallas_call(
        attend_kernel,
        out_shape=(
            jax.ShapeDtypeStruct((2, quarter, width), jnp.bfloat16),
            jax.ShapeDtypeStruct((2, quarter, width), jnp.float32),
        ),
        in_specs=[SMEM, SMEM, VMEM, VMEM],
        out_specs=(VMEM, VMEM),
        compiler_params=pltpu.CompilerParams(vmem_limit_bytes=16 << 20),
        name="attend",
    )(place, first, context, w_out)


def norm_kernel(
    place_ref,
    keep_ref,
    lower_ref,
    upper_ref,
    resid_ref,
    gain_ref,
    ids_ref,
    router_ref,
    slot_hot_ref,
    middle_ref,
    row_ref,
):
    attention = (
        keep_ref[0] + lower_ref[0].astype(jnp.float32) + upper_ref[...].astype(jnp.float32)
    )
    middle = resid_ref[...].astype(jnp.float32) + attention
    middle_ref[...] = middle
    width = middle.shape[1]
    normed = rms_scaled(middle, gain_ref[...]).astype(jnp.bfloat16)
    row_ref[:, :width] = normed
    logits = jnp.dot(normed, router_ref[...], preferred_element_type=jnp.float32)
    expert = lax.broadcasted_iota(jnp.int32, logits.shape, 1)
    ids = ids_ref[...]
    hit = ids[:, 0:1] == expert
    for choice in range(1, ids.shape[1]):
        hit = hit | (ids[:, choice : choice + 1] == expert)
    raised = jnp.where(hit, jnp.exp(logits), 0.0)
    weights = (raised / jnp.sum(raised, axis=1, keepdims=True)).astype(jnp.bfloat16)
    row_ref[:, width:] = jnp.dot(
        weights, slot_hot_ref[...], preferred_element_type=jnp.float32
    ).astype(jnp.bfloat16)


def norm_rows(place, keep, from_lower, from_upper, resid, gain, ids, router, slot_hot, number):
    rows, width = from_upper.shape
    chunks = keep.shape[1] // rows
    extra = slot_hot.shape[1]

    def whole(array):
        return pl.BlockSpec(array.shape, lambda i, p: (0, 0))

    def mine(array):
        return pl.BlockSpec((rows, array.shape[1]), lambda i, p: (p[0] * chunks + number, 0))

    return pl.pallas_call(
        norm_kernel,
        out_shape=(
            jax.ShapeDtypeStruct((rows, width), jnp.float32),
            jax.ShapeDtypeStruct((rows, width + extra), jnp.bfloat16),
        ),
        grid_spec=pltpu.PrefetchScalarGridSpec(
            num_scalar_prefetch=1,
            grid=(1,),
            in_specs=[
                pl.BlockSpec((1, rows, width), lambda i, p: (0, number, 0)),
                pl.BlockSpec((1, rows, width), lambda i, p: (0, number, 0)),
                whole(from_upper),
                mine(resid),
                whole(gain),
                mine(ids),
                whole(router),
                whole(slot_hot),
            ],
            out_specs=[
                pl.BlockSpec((rows, width), lambda i, p: (0, 0)),
                pl.BlockSpec((rows, width + extra), lambda i, p: (0, 0)),
            ],
        ),
        compiler_params=pltpu.CompilerParams(vmem_limit_bytes=16 << 20),
        name="norm_rows",
    )(place, keep, from_lower, from_upper, resid, gain, ids, router, slot_hot)


def load_kernel(gate_hbm, up_hbm, down_hbm, both_ref, down_ref, mark_ref, sems):
    units = gate_hbm.shape[2]
    copies = [
        pltpu.make_async_copy(gate_hbm, both_ref.at[:, :, pl.ds(0, units)], sems.at[0]),
        pltpu.make_async_copy(up_hbm, both_ref.at[:, :, pl.ds(units, units)], sems.at[1]),
        pltpu.make_async_copy(down_hbm, down_ref, sems.at[2]),
    ]
    for copy in copies:
        copy.start()
    mark_ref[...] = jnp.zeros_like(mark_ref)
    for copy in copies:
        copy.wait()


def load_weights(w_gate, w_up, w_down):
    held, width, units = w_gate.shape
    return pl.pallas_call(
        load_kernel,
        out_shape=(
            pltpu.VMEM((held, width, 2 * units), jnp.bfloat16),
            pltpu.VMEM((held * units, width), jnp.bfloat16),
            jax.ShapeDtypeStruct((8, LANES), jnp.int32),
        ),
        in_specs=[ANY] * 3,
        out_specs=(VMEM, VMEM, VMEM),
        scratch_shapes=[pltpu.SemaphoreType.DMA((3,))],
        compiler_params=pltpu.CompilerParams(vmem_limit_bytes=2 << 20),
        name="load_weights",
    )(w_gate, w_up, w_down)


def expert_kernel(
    first_ref,
    near_ref,
    far_ref,
    both_ref,
    down_ref,
    loaded_hbm,
    near_out,
    far_out,
    hidden_ref,
):
    held, width, units = both_ref.shape
    units = units // 2
    extra = near_ref.shape[1] - width
    mine = lax.broadcasted_iota(jnp.int32, (extra, LANES), 1) + first_ref[0]
    mine = (lax.broadcasted_iota(jnp.int32, (extra, LANES), 0) == mine).astype(jnp.bfloat16)
    tile = 512 if width % 512 == 0 else width
    start = 0
    spans = []
    for piece, out in ((near_ref, near_out), (far_ref, far_out)):
        block = min(ROW_BLOCK, piece.shape[0])
        for at in range(0, piece.shape[0], block):
            spans.append((piece, out, pl.ds(at, block), pl.ds(start + at, block)))
        start += piece.shape[0]
    scales = [
        jnp.dot(piece[at, width:], mine, preferred_element_type=jnp.float32)
        for piece, out, at, to in spans
    ]
    for slot in range(held):
        for (piece, _, at, to), weights in zip(spans, scales):
            out = jnp.dot(piece[at, :width], both_ref[slot], preferred_element_type=jnp.float32)
            gate, upper = out[:, :units], out[:, units:]
            hidden = jax.nn.silu(gate) * upper * weights[:, slot : slot + 1]
            hidden_ref[to, slot * units : (slot + 1) * units] = hidden.astype(jnp.bfloat16)
    for left in range(0, width, tile):
        for _, out_ref, at, to in spans:
            out_ref[at, left : left + tile] = jnp.dot(
                hidden_ref[to, :], down_ref[:, left : left + tile], preferred_element_type=jnp.float32
            ).astype(jnp.bfloat16)


def expert_rows(first, pieces, both, down, loaded):
    held, width, units = both.shape
    units = units // 2
    rows = sum(p.shape[0] for p in pieces)
    return pl.pallas_call(
        expert_kernel,
        out_shape=[jax.ShapeDtypeStruct((p.shape[0], width), jnp.bfloat16) for p in pieces],
        in_specs=[SMEM] + [VMEM] * (len(pieces) + 2) + [ANY],
        out_specs=[VMEM] * len(pieces),
        scratch_shapes=[
            pltpu.VMEM((rows, held * units), jnp.bfloat16),
        ],
        compiler_params=pltpu.CompilerParams(vmem_limit_bytes=32 << 20),
        cost_estimate=pl.CostEstimate(
            flops=6 * rows * width * held * units,
            bytes_accessed=4 * rows * width + 6 * held * width * units,
            transcendentals=rows * held * units,
        ),
        name="expert_rows",
    )(first, *pieces, both, down, loaded)


def wide(value):
    return value.astype(jnp.float32)


def short(value):
    return value.astype(jnp.bfloat16)


def after(value, *others):
    return lax.optimization_barrier((value, others))[0]


def cut(value, start, size):
    return wide(lax.slice_in_dim(value, start, start + size, axis=0))


class Chunk:
    def __init__(self, rows):
        self.rows = rows
        self.outer = lax.axis_size("ep") // 2
        self.half = rows.shape[0] // 2

    def gather_outer(self, *then):
        rows = after(self.rows, *then)
        ring = [rows] + [turn(rows, step) for step in range(1, self.outer)]
        self.first = jnp.concatenate([r[: self.half] for r in ring], axis=0)
        self.second = jnp.concatenate([r[self.half :] for r in ring], axis=0)

    def gather_near(self, *then):
        first, second = after(self.first, *then), after(self.second, *then)
        inner, upper = lax.optimization_barrier((flip_inner(first), flip_upper(second)))
        self.first = jnp.concatenate([first, inner], axis=0)
        self.second = jnp.concatenate([second, upper], axis=0)

    def gather_far(self):
        self.far_pair = flip_upper(self.first), flip_inner(self.second)

    def gathered_far(self, *then):
        self.pieces = [
            jnp.concatenate([self.first, self.second], axis=0),
            jnp.concatenate(after(self.far_pair, *then), axis=0),
        ]

    def gather_lower(self, *then):
        self.others = [flip_lower(after(p, *then)) for p in self.pieces]

    def back_lower(self):
        self.got = [flip_lower(p) for p in self.away]

    def two(self, number, start, size):
        return cut(self.own[number], start, size) + cut(self.got[number], start, size)

    def back_far(self):
        size = self.own[0].shape[0] // 2
        self.far = short(self.two(1, 0, size)), short(self.two(1, size, size))
        self.far_first, self.far_second = flip_upper(self.far[0]), flip_inner(self.far[1])

    def back_near(self):
        part = self.own[0].shape[0] // 2
        size = part // 2
        first = short(self.two(0, size, size) + cut(self.far_first, size, size))
        second = short(self.two(0, part + size, size) + cut(self.far_second, size, size))
        self.near = first, second
        self.near_first, self.near_second = flip_inner(first), flip_upper(second)

    def block(self, number):
        at, size, part = number * self.half, self.half, self.own[0].shape[0] // 2
        first = self.two(0, at, size) + cut(self.far_first, at, size)
        second = self.two(0, part + at, size) + cut(self.far_second, at, size)
        first = first + cut(self.near_first, at, size)
        second = second + cut(self.near_second, at, size)
        return jnp.concatenate([first, second], axis=0)

    def back_outer(self):
        self.total = self.block(0)
        self.turned = [turn(short(self.block(k)), -k) for k in range(1, self.outer)]

    def finish(self, middle, gain, *then):
        total = middle + self.total
        for turned in after(self.turned, *then):
            total = total + wide(turned)
        return rms_scaled(total, gain).astype(jnp.bfloat16)


def spread(rows):
    size = lax.axis_size("tp")
    both = lax.ppermute(rows, "tp", [(i, i ^ 3) for i in range(size)])
    return [rows, flip_lower(rows), flip_upper(rows), both]


def join_kernel(place_ref, *refs):
    last_ref, out_ref = refs[-2:]
    quarter = out_ref.shape[0] // 4
    size = refs[0].shape[0]
    for number, piece in enumerate(refs[:-2]):
        start = (place_ref[0] ^ number) * quarter
        out_ref[pl.ds(pl.multiple_of(start, size), size), :] = piece[...]
        out_ref[number * quarter + size : (number + 1) * quarter, :] = last_ref[number]


def join(place, pieces, last):
    rows, width = pieces[0].shape
    return pl.pallas_call(
        join_kernel,
        out_shape=jax.ShapeDtypeStruct((rows * 4 * CHUNKS, width), pieces[0].dtype),
        in_specs=[SMEM] + [VMEM] * (len(pieces) + 1),
        out_specs=VMEM,
        compiler_params=pltpu.CompilerParams(vmem_limit_bytes=16 << 20),
        name="join",
    )(place, *pieces, last)


def local(
    resid,
    context,
    w_out,
    pre_gain,
    final_gain,
    w_router,
    expert_ids,
    slot_expert,
    copy_pick,
    w_gate,
    w_up,
    w_down,
):
    held, width, units = w_gate.shape
    row_count = resid.shape[0]
    experts = w_router.shape[1]
    slots = slot_expert.shape[0]
    quarter = row_count // 4
    rows = quarter // CHUNKS
    place = lax.axis_index("tp").astype(jnp.int32).reshape(1)
    first = (lax.axis_index("ep") * held).astype(jnp.int32).reshape(1)
    down = w_down.reshape(held * units, width)

    send, keep = attend(place, first, context, w_out)
    got = flip_lower(send)
    parts = []
    for number in range(CHUNKS):
        at = slice(number * rows, (number + 1) * rows)
        parts.append(short(keep[1, at] + wide(got[1, at])))
    table = slot_of_pick(after(slot_expert, parts[0]), copy_pick, experts)[0]
    lanes = -(-slots // LANES) * LANES
    slot_hot = table[:, None] == jnp.arange(lanes, dtype=jnp.int32)[None, :]
    slot_hot = slot_hot.astype(jnp.bfloat16)

    gain = pre_gain.reshape(1, -1)
    uppers = [flip_upper(part) for part in parts]
    middles, chunks = [], []
    for number in range(CHUNKS):
        middle, row = norm_rows(
            place, keep, got, uppers[number], resid, gain, expert_ids, w_router, slot_hot, number
        )
        middles.append(middle)
        chunks.append(Chunk(row))

    both, down, loaded = load_weights(w_gate, w_up, after(down, uppers))

    def serve(pieces, *then):
        return expert_rows(first, [after(p, *then) for p in pieces], both, down, loaded)

    one, two = chunks
    one.gather_outer()
    one.first, one.second = after((one.first, one.second), loaded)
    one.gather_near()
    two.gather_outer(one.first)
    one.gather_far()
    two.gather_near()
    one.gathered_far()
    one.gather_lower(one.pieces[1])
    two.gather_far()
    one.away = serve(one.others)
    one.back_lower()
    one.own = serve(one.pieces, one.away)
    two.gathered_far(one.own)
    two.gather_lower()
    one.back_far()
    two.away = serve(two.others, one.far)
    two.back_lower()
    two.own = serve(two.pieces, two.away)
    one.far_first, one.far_second = after((one.far_first, one.far_second), two.own)
    one.back_near()
    two.back_far()
    one.near_first, one.near_second = after((one.near_first, one.near_second), two.far)
    one.back_outer()
    two.back_near()
    two.back_outer()
    result_one = one.finish(middles[0], final_gain, two.near)
    ready_one = spread(result_one)
    result_two = two.finish(middles[1], final_gain, result_one)
    return join(place, ready_one, lax.all_gather(result_two, "tp"))


def solution(mesh):
    return jax.shard_map(
        local,
        mesh=mesh,
        in_specs=(
            P("ep", None),
            P("ep", "tp"),
            P("tp", None),
            P(),
            P(),
            P(),
            P("ep", None),
            P(),
            P("ep", None),
            P("ep", None, "tp"),
            P("ep", None, "tp"),
            P("ep", "tp", None),
        ),
        out_specs=P("ep", None),
        check_vma=False,
    )
```

```python
import functools

import jax
import jax.numpy as jnp
from jax import lax
from jax.experimental import pallas as pl
from jax.experimental.pallas import tpu as pltpu
from jax.sharding import PartitionSpec as P

EPSILON = 1e-06
CHUNKS = 2
LANES = 128
ROW_BLOCK = 512


def slot_of_pick(slot_expert, copy_pick, experts):
    count = slot_expert.shape[0]
    order = jnp.arange(count, dtype=jnp.int32)
    same = slot_expert[:, None] == slot_expert[None, :]
    before = order[None, :] < order[:, None]
    rank = jnp.sum((same & before).astype(jnp.int32), axis=1)
    holds = slot_expert[None, :] == jnp.arange(experts, dtype=jnp.int32)[:, None]
    copies = jnp.sum(holds.astype(jnp.int32), axis=1)
    wanted = copy_pick % copies[None, :]
    match = holds[None, :, :] & (rank[None, None, :] == wanted[:, :, None])
    return jnp.sum(match.astype(jnp.int32) * order[None, None, :], axis=2)


def rms_scaled(values, gain):
    mean_square = jnp.mean(values * values, axis=-1, keepdims=True)
    return values * lax.rsqrt(mean_square + EPSILON) * gain.astype(jnp.float32)


def turn(value, step):
    count = lax.axis_size("ep")
    return lax.ppermute(value, "ep", [(i, (i + 2 * step) % count) for i in range(count)])


def flip_inner(value):
    return lax.ppermute(value, "ep", [(i, i ^ 1) for i in range(lax.axis_size("ep"))])


def flip_upper(value):
    return lax.ppermute(value, "tp", [(i, i ^ 2) for i in range(lax.axis_size("tp"))])


def flip_lower(value):
    return lax.ppermute(value, "tp", [(i, i ^ 1) for i in range(lax.axis_size("tp"))])


VMEM = pl.BlockSpec(memory_space=pltpu.VMEM)
SMEM = pl.BlockSpec(memory_space=pltpu.SMEM)
ANY = pl.BlockSpec(memory_space=pl.ANY)


def attend_kernel(place_ref, first_ref, context_ref, w_ref, send_ref, keep_ref):
    quarter = send_ref.shape[1]
    rows = context_ref[...]
    width = w_ref.shape[1]
    tile = 512 if width % 512 == 0 else width
    for left in range(0, width, tile):
        out = jnp.dot(rows, w_ref[:, left : left + tile], preferred_element_type=jnp.float32)
        for upper in (0, 1):
            send_ref[upper, :, left : left + tile] = out[
                upper * quarter : (upper + 1) * quarter
            ].astype(jnp.bfloat16)
            keep_ref[upper, :, left : left + tile] = out[
                (upper + 2) * quarter : (upper + 3) * quarter
            ]


def attend(place, first, context, w_out):
    rows, _ = context.shape
    width = w_out.shape[1]
    quarter = rows // 4
    return pl.pallas_call(
        attend_kernel,
        out_shape=(
            jax.ShapeDtypeStruct((2, quarter, width), jnp.bfloat16),
            jax.ShapeDtypeStruct((2, quarter, width), jnp.float32),
        ),
        in_specs=[SMEM, SMEM, VMEM, VMEM],
        out_specs=(VMEM, VMEM),
        compiler_params=pltpu.CompilerParams(vmem_limit_bytes=16 << 20),
        name="attend",
    )(place, first, context, w_out)


def norm_kernel(
    place_ref,
    keep_ref,
    lower_ref,
    upper_ref,
    resid_ref,
    gain_ref,
    ids_ref,
    router_ref,
    slot_hot_ref,
    middle_ref,
    row_ref,
):
    attention = (
        keep_ref[0] + lower_ref[0].astype(jnp.float32) + upper_ref[...].astype(jnp.float32)
    )
    middle = resid_ref[...].astype(jnp.float32) + attention
    middle_ref[...] = middle
    width = middle.shape[1]
    normed = rms_scaled(middle, gain_ref[...]).astype(jnp.bfloat16)
    row_ref[:, :width] = normed
    logits = jnp.dot(normed, router_ref[...], preferred_element_type=jnp.float32)
    expert = lax.broadcasted_iota(jnp.int32, logits.shape, 1)
    ids = ids_ref[...]
    hit = ids[:, 0:1] == expert
    for choice in range(1, ids.shape[1]):
        hit = hit | (ids[:, choice : choice + 1] == expert)
    raised = jnp.where(hit, jnp.exp(logits), 0.0)
    weights = (raised / jnp.sum(raised, axis=1, keepdims=True)).astype(jnp.bfloat16)
    row_ref[:, width:] = jnp.dot(
        weights, slot_hot_ref[...], preferred_element_type=jnp.float32
    ).astype(jnp.bfloat16)


def norm_rows(place, keep, from_lower, from_upper, resid, gain, ids, router, slot_hot, number):
    rows, width = from_upper.shape
    chunks = keep.shape[1] // rows
    extra = slot_hot.shape[1]

    def whole(array):
        return pl.BlockSpec(array.shape, lambda i, p: (0, 0))

    def mine(array):
        return pl.BlockSpec((rows, array.shape[1]), lambda i, p: (p[0] * chunks + number, 0))

    return pl.pallas_call(
        norm_kernel,
        out_shape=(
            jax.ShapeDtypeStruct((rows, width), jnp.float32),
            jax.ShapeDtypeStruct((rows, width + extra), jnp.bfloat16),
        ),
        grid_spec=pltpu.PrefetchScalarGridSpec(
            num_scalar_prefetch=1,
            grid=(1,),
            in_specs=[
                pl.BlockSpec((1, rows, width), lambda i, p: (0, number, 0)),
                pl.BlockSpec((1, rows, width), lambda i, p: (0, number, 0)),
                whole(from_upper),
                mine(resid),
                whole(gain),
                mine(ids),
                whole(router),
                whole(slot_hot),
            ],
            out_specs=[
                pl.BlockSpec((rows, width), lambda i, p: (0, 0)),
                pl.BlockSpec((rows, width + extra), lambda i, p: (0, 0)),
            ],
        ),
        compiler_params=pltpu.CompilerParams(vmem_limit_bytes=16 << 20),
        name="norm_rows",
    )(place, keep, from_lower, from_upper, resid, gain, ids, router, slot_hot)


def load_kernel(gate_hbm, up_hbm, down_hbm, both_ref, down_ref, mark_ref, sems):
    units = gate_hbm.shape[2]
    copies = [
        pltpu.make_async_copy(gate_hbm, both_ref.at[:, :, pl.ds(0, units)], sems.at[0]),
        pltpu.make_async_copy(up_hbm, both_ref.at[:, :, pl.ds(units, units)], sems.at[1]),
        pltpu.make_async_copy(down_hbm, down_ref, sems.at[2]),
    ]
    for copy in copies:
        copy.start()
    mark_ref[...] = jnp.zeros_like(mark_ref)
    for copy in copies:
        copy.wait()


def load_weights(w_gate, w_up, w_down):
    held, width, units = w_gate.shape
    return pl.pallas_call(
        load_kernel,
        out_shape=(
            pltpu.VMEM((held, width, 2 * units), jnp.bfloat16),
            pltpu.VMEM((held * units, width), jnp.bfloat16),
            jax.ShapeDtypeStruct((8, LANES), jnp.int32),
        ),
        in_specs=[ANY] * 3,
        out_specs=(VMEM, VMEM, VMEM),
        scratch_shapes=[pltpu.SemaphoreType.DMA((3,))],
        compiler_params=pltpu.CompilerParams(vmem_limit_bytes=2 << 20),
        name="load_weights",
    )(w_gate, w_up, w_down)


def expert_kernel(
    first_ref,
    near_ref,
    far_ref,
    both_ref,
    down_ref,
    loaded_hbm,
    near_out,
    far_out,
    hidden_ref,
):
    held, width, units = both_ref.shape
    units = units // 2
    extra = near_ref.shape[1] - width
    mine = lax.broadcasted_iota(jnp.int32, (extra, LANES), 1) + first_ref[0]
    mine = (lax.broadcasted_iota(jnp.int32, (extra, LANES), 0) == mine).astype(jnp.bfloat16)
    tile = 512 if width % 512 == 0 else width
    start = 0
    spans = []
    for piece, out in ((near_ref, near_out), (far_ref, far_out)):
        block = min(ROW_BLOCK, piece.shape[0])
        for at in range(0, piece.shape[0], block):
            spans.append((piece, out, pl.ds(at, block), pl.ds(start + at, block)))
        start += piece.shape[0]
    scales = [
        jnp.dot(piece[at, width:], mine, preferred_element_type=jnp.float32)
        for piece, out, at, to in spans
    ]
    for slot in range(held):
        for (piece, _, at, to), weights in zip(spans, scales):
            out = jnp.dot(piece[at, :width], both_ref[slot], preferred_element_type=jnp.float32)
            gate, upper = out[:, :units], out[:, units:]
            hidden = jax.nn.silu(gate) * upper * weights[:, slot : slot + 1]
            hidden_ref[to, slot * units : (slot + 1) * units] = hidden.astype(jnp.bfloat16)
    for left in range(0, width, tile):
        for _, out_ref, at, to in spans:
            out_ref[at, left : left + tile] = jnp.dot(
                hidden_ref[to, :], down_ref[:, left : left + tile], preferred_element_type=jnp.float32
            ).astype(jnp.bfloat16)


def expert_rows(first, pieces, both, down, loaded):
    held, width, units = both.shape
    units = units // 2
    rows = sum(p.shape[0] for p in pieces)
    return pl.pallas_call(
        expert_kernel,
        out_shape=[jax.ShapeDtypeStruct((p.shape[0], width), jnp.bfloat16) for p in pieces],
        in_specs=[SMEM] + [VMEM] * (len(pieces) + 2) + [ANY],
        out_specs=[VMEM] * len(pieces),
        scratch_shapes=[
            pltpu.VMEM((rows, held * units), jnp.bfloat16),
        ],
        compiler_params=pltpu.CompilerParams(vmem_limit_bytes=32 << 20),
        cost_estimate=pl.CostEstimate(
            flops=6 * rows * width * held * units,
            bytes_accessed=4 * rows * width + 6 * held * width * units,
            transcendentals=rows * held * units,
        ),
        name="expert_rows",
    )(first, *pieces, both, down, loaded)


def wide(value):
    return value.astype(jnp.float32)


def short(value):
    return value.astype(jnp.bfloat16)


def after(value, *others):
    return lax.optimization_barrier((value, others))[0]


def cut(value, start, size):
    return wide(lax.slice_in_dim(value, start, start + size, axis=0))


class Chunk:
    def __init__(self, rows):
        self.rows = rows
        self.outer = lax.axis_size("ep") // 2
        self.half = rows.shape[0] // 2

    def gather_outer(self, *then):
        rows = after(self.rows, *then)
        ring = [rows] + [turn(rows, step) for step in range(1, self.outer)]
        self.first = jnp.concatenate([r[: self.half] for r in ring], axis=0)
        self.second = jnp.concatenate([r[self.half :] for r in ring], axis=0)

    def gather_near(self, *then):
        first, second = after(self.first, *then), after(self.second, *then)
        inner, upper = lax.optimization_barrier((flip_inner(first), flip_upper(second)))
        self.first = jnp.concatenate([first, inner], axis=0)
        self.second = jnp.concatenate([second, upper], axis=0)

    def gather_far(self):
        self.far_pair = flip_upper(self.first), flip_inner(self.second)

    def gathered_far(self, *then):
        self.pieces = [
            jnp.concatenate([self.first, self.second], axis=0),
            jnp.concatenate(after(self.far_pair, *then), axis=0),
        ]

    def gather_lower(self, *then):
        self.others = [flip_lower(after(p, *then)) for p in self.pieces]

    def back_lower(self):
        self.got = [flip_lower(p) for p in self.away]

    def two(self, number, start, size):
        return cut(self.own[number], start, size) + cut(self.got[number], start, size)

    def back_far(self):
        size = self.own[0].shape[0] // 2
        self.far = short(self.two(1, 0, size)), short(self.two(1, size, size))
        self.far_first, self.far_second = flip_upper(self.far[0]), flip_inner(self.far[1])

    def back_near(self):
        part = self.own[0].shape[0] // 2
        size = part // 2
        first = short(self.two(0, size, size) + cut(self.far_first, size, size))
        second = short(self.two(0, part + size, size) + cut(self.far_second, size, size))
        self.near = first, second
        self.near_first, self.near_second = flip_inner(first), flip_upper(second)

    def block(self, number):
        at, size, part = number * self.half, self.half, self.own[0].shape[0] // 2
        first = self.two(0, at, size) + cut(self.far_first, at, size)
        second = self.two(0, part + at, size) + cut(self.far_second, at, size)
        first = first + cut(self.near_first, at, size)
        second = second + cut(self.near_second, at, size)
        return jnp.concatenate([first, second], axis=0)

    def back_outer(self):
        self.total = self.block(0)
        self.turned = [turn(short(self.block(k)), -k) for k in range(1, self.outer)]

    def finish(self, middle, gain, *then):
        total = middle + self.total
        for turned in after(self.turned, *then):
            total = total + wide(turned)
        return rms_scaled(total, gain).astype(jnp.bfloat16)


def spread(rows):
    size = lax.axis_size("tp")
    both = lax.ppermute(rows, "tp", [(i, i ^ 3) for i in range(size)])
    return [rows, flip_lower(rows), flip_upper(rows), both]


def join_kernel(place_ref, *refs):
    last_ref, out_ref = refs[-2:]
    quarter = out_ref.shape[0] // 4
    size = refs[0].shape[0]
    for number, piece in enumerate(refs[:-2]):
        start = (place_ref[0] ^ number) * quarter
        out_ref[pl.ds(pl.multiple_of(start, size), size), :] = piece[...]
        out_ref[number * quarter + size : (number + 1) * quarter, :] = last_ref[number]


def join(place, pieces, last):
    rows, width = pieces[0].shape
    return pl.pallas_call(
        join_kernel,
        out_shape=jax.ShapeDtypeStruct((rows * 4 * CHUNKS, width), pieces[0].dtype),
        in_specs=[SMEM] + [VMEM] * (len(pieces) + 1),
        out_specs=VMEM,
        compiler_params=pltpu.CompilerParams(vmem_limit_bytes=16 << 20),
        name="join",
    )(place, *pieces, last)


def local(
    resid,
    context,
    w_out,
    pre_gain,
    final_gain,
    w_router,
    expert_ids,
    slot_expert,
    copy_pick,
    w_gate,
    w_up,
    w_down,
):
    held, width, units = w_gate.shape
    row_count = resid.shape[0]
    experts = w_router.shape[1]
    slots = slot_expert.shape[0]
    quarter = row_count // 4
    rows = quarter // CHUNKS
    place = lax.axis_index("tp").astype(jnp.int32).reshape(1)
    first = (lax.axis_index("ep") * held).astype(jnp.int32).reshape(1)
    down = w_down.reshape(held * units, width)

    index = lax.axis_index("tp")
    blocks = context.reshape(2, 2, quarter, context.shape[1])
    blocks = jnp.where(index // 2 == 1, blocks[::-1], blocks)
    blocks = jnp.where(index % 2 == 0, blocks[:, ::-1], blocks)
    context = jnp.swapaxes(blocks, 0, 1).reshape(context.shape)
    send, keep = attend(place, first, context, w_out)
    got = flip_lower(send)
    parts = []
    for number in range(CHUNKS):
        at = slice(number * rows, (number + 1) * rows)
        parts.append(short(keep[1, at] + wide(got[1, at])))
    table = slot_of_pick(after(slot_expert, parts[0]), copy_pick, experts)[0]
    lanes = -(-slots // LANES) * LANES
    slot_hot = table[:, None] == jnp.arange(lanes, dtype=jnp.int32)[None, :]
    slot_hot = slot_hot.astype(jnp.bfloat16)

    gain = pre_gain.reshape(1, -1)
    uppers = [flip_upper(part) for part in parts]
    middles, chunks = [], []
    for number in range(CHUNKS):
        middle, row = norm_rows(
            place, keep, got, uppers[number], resid, gain, expert_ids, w_router, slot_hot, number
        )
        middles.append(middle)
        chunks.append(Chunk(row))

    both, down, loaded = load_weights(w_gate, w_up, after(down, uppers))

    def serve(pieces, *then):
        return expert_rows(first, [after(p, *then) for p in pieces], both, down, loaded)

    one, two = chunks
    one.gather_outer()
    one.first, one.second = after((one.first, one.second), loaded)
    one.gather_near()
    two.gather_outer(one.first)
    one.gather_far()
    two.gather_near()
    one.gathered_far()
    one.gather_lower()
    two.gather_far()
    one.away = serve(one.others)
    one.back_lower()
    one.own = serve(one.pieces, one.away)
    two.gathered_far(one.own)
    two.gather_lower()
    one.back_far()
    two.away = serve(two.others, one.far)
    two.back_lower()
    two.own = serve(two.pieces, two.away)
    one.back_near()
    two.back_far()
    one.near_first, one.near_second = after((one.near_first, one.near_second), two.far)
    one.back_outer()
    two.back_near()
    two.back_outer()
    result_one = one.finish(middles[0], final_gain, two.near)
    ready_one = spread(result_one)
    result_two = two.finish(middles[1], final_gain, result_one)
    return join(place, ready_one, lax.all_gather(result_two, "tp"))


def solution(mesh):
    return jax.shard_map(
        local,
        mesh=mesh,
        in_specs=(
            P("ep", None),
            P("ep", "tp"),
            P("tp", None),
            P(),
            P(),
            P(),
            P("ep", None),
            P(),
            P("ep", None),
            P("ep", None, "tp"),
            P("ep", None, "tp"),
            P("ep", "tp", None),
        ),
        out_specs=P("ep", None),
        check_vma=False,
    )
```
